128 devices in a mesh: dp: 8 (over x_lo, z), tensor: 16 (over x_hi, y, core).
Axes of the slice: x: 4 (x_hi: 2, x_lo: 2; x = x_hi * 2 + x_lo), y: 4, z: 4, core: 2. Of those that a mesh axis runs over, the one named last changes fastest.
Arguments:
- tokens: bfloat16 [8, 2048, 4096], P('dp', 'tensor'), may hold values from -1.8 to 1.8
- cotangent: bfloat16 [8, 2048, 4096], P('dp', None, 'tensor'), may hold values from -6 to 6
- gain: float32 [4096], replicated, may hold values from 0.25 to 3.5
- w_query: bfloat16 [4096, 4096], P(None, 'tensor'), may hold values from -6 to 6
- w_key: bfloat16 [4096, 512], P(None, 'tensor'), may hold values from -6 to 6
- w_value: bfloat16 [4096, 512], P(None, 'tensor'), may hold values from -6 to 6
- moment_query: float32 [4096, 4096], P('dp', 'tensor'), may hold values from -6 to 6
- moment_key: float32 [4096, 512], P('dp', 'tensor'), may hold values from -6 to 6
- moment_value: float32 [4096, 512], P('dp', 'tensor'), may hold values from -6 to 6
Outputs:
- attended: bfloat16 [8, 2048, 4096], P('dp', None, 'tensor')
- grad_tokens: bfloat16 [8, 2048, 4096], P('dp', 'tensor')
- fresh_query: bfloat16 [4096, 4096], P(None, 'tensor')
- fresh_key: bfloat16 [4096, 512], P(None, 'tensor')
- fresh_value: bfloat16 [4096, 512], P(None, 'tensor')
- next_query: float32 [4096, 4096], P('dp', 'tensor')
- next_key: float32 [4096, 512], P('dp', 'tensor')
- next_value: float32 [4096, 512], P('dp', 'tensor')
The draws below stay inside these ranges and needn't reach their ends.
All inputs are finite; a program needn't handle non-finite values.
Results may differ from the reference program's by a relative error of at most 0.017.
Values may be sent and summed in bfloat16 or wider, within the bound.
A program may use at most 256 MiB of HBM per device.

```python
import jax
import jax.numpy as jnp
from jax import lax

D = 4096
HEADS = 32
KVH = 4
HD = 128
SEQ = 2048
SEQS = 8
N_TENSOR = 16


def drawn_weight(key, columns, salt):
    base = jnp.clip(jax.random.normal(jax.random.fold_in(key, salt), (D, columns), jnp.float32), -6.0, 6.0)
    return base


def draw_tokens(key, part):
    noise = jax.random.normal(jax.random.fold_in(key, 21), (SEQS, SEQ, D), jnp.float32)
    values = 0.3 * noise
    return jnp.clip(values, -1.8, 1.8).astype(jnp.bfloat16)


def draw_gain(key, part):
    spot = jnp.arange(D, dtype=jnp.float32) / (D - 1.0)
    rough = jax.random.uniform(jax.random.fold_in(key, 31), (D,), jnp.float32, 0.85, 1.15)
    trend = 0.5 + spot
    return trend * rough


def draw_w_query(key, part):
    return drawn_weight(key, HEADS * HD, 11).astype(jnp.bfloat16)


def draw_w_key(key, part):
    return drawn_weight(key, KVH * HD, 12).astype(jnp.bfloat16)


def block_levels(own_key, dims, shards, low, high):
    level = 1.0
    for position, parts in shards:
        steps = jax.random.uniform(jax.random.fold_in(jax.random.fold_in(own_key, 6), position), (parts,), jnp.float32, low / len(shards), high / len(shards))
        level = level * jnp.repeat(jnp.exp(steps), dims[position] // parts).reshape((-1,) + (1,) * (len(dims) - 1 - position))
    return level


def centred(rng, dims, scale, most, cuts=(), kind=jnp.bfloat16):
    result = scale * jax.random.normal(rng, dims, jnp.float32)
    if cuts:
        result = result * block_levels(rng, dims, cuts, -0.22, 0.18)
    return jnp.clip(result, -most, most).astype(kind)


def setup_inputs(seed: int = 0) -> dict:
    seeds = jax.random.split(jax.random.key(seed), 10)
    return {
        "tokens": draw_tokens(jax.random.fold_in(seeds[9], 71), 0),
        "cotangent": centred(seeds[1], (SEQS, SEQ, HEADS * HD), 1.0, 6.0, ((0, 8), (2, 16))),
        "gain": draw_gain(jax.random.fold_in(seeds[9], 71), 0),
        "w_query": draw_w_query(jax.random.fold_in(seeds[9], 71), 0),
        "w_key": draw_w_key(jax.random.fold_in(seeds[9], 71), 0),
        "w_value": centred(seeds[5], (D, KVH * HD), 1.0, 6.0, ((1, 16),)),
        "moment_query": centred(seeds[6], (D, HEADS * HD), 1.0, 6.0, ((0, 8), (1, 16)), jnp.float32),
        "moment_key": centred(seeds[7], (D, KVH * HD), 1.0, 6.0, ((0, 8), (1, 16)), jnp.float32),
        "moment_value": centred(seeds[8], (D, KVH * HD), 1.0, 6.0, ((0, 8), (1, 16)), jnp.float32),
    }


rope_base = 1000000.0
norm_eps = 1e-06
stat_eps = 1e-06
learn_rate = 0.05
keep_rate = 0.9

def rotate(matrix, first_column, head_size, sign):
    length = matrix.shape[0]
    columns = matrix.shape[1]
    index = first_column + jnp.arange(columns, dtype=jnp.int32)
    within = index % head_size // 2
    rates = jnp.power(jnp.float32(rope_base), within.astype(jnp.float32) * (-2.0 / head_size))
    angle = jnp.arange(length, dtype=jnp.float32)[:, None] * rates[None, :]
    even = index % 2 == 0
    partner = jnp.where(even[None, :], -jnp.roll(matrix, -1, axis=1), jnp.roll(matrix, 1, axis=1))
    return matrix * jnp.cos(angle) + partner * (sign * jnp.sin(angle))

def settle(values):
    return lax.optimization_barrier(values.astype(jnp.bfloat16)).astype(jnp.float32)

def split_columns(matrix, count):
    return matrix.reshape(matrix.shape[0], N_TENSOR, count).transpose(1, 0, 2)

def sequence_pass(tokens_one, grad_one, gain, w_query, w_key, w_value):
    length = tokens_one.shape[0]
    width = tokens_one.shape[1]
    group = HEADS // KVH
    per_device = HEADS // N_TENSOR
    blocks = group // per_device
    in_scale = width ** (-0.5)
    head_scale = HD ** (-0.5)
    inputs = tokens_one.astype(jnp.float32)
    reciprocal = lax.rsqrt(lax.optimization_barrier(jnp.mean(inputs * inputs, axis=1, keepdims=True)) + norm_eps)
    unit_rows = inputs * reciprocal
    normed = (unit_rows * gain).astype(jnp.bfloat16)
    query = rotate(jnp.dot(normed, w_query, preferred_element_type=jnp.float32) * in_scale, 0, HD, 1.0).astype(jnp.bfloat16)
    keys = rotate(jnp.dot(normed, w_key, preferred_element_type=jnp.float32) * in_scale, 0, HD, 1.0).astype(jnp.bfloat16)
    values = (jnp.dot(normed, w_value, preferred_element_type=jnp.float32) * in_scale).astype(jnp.bfloat16)
    query_groups = query.reshape(length, KVH, group, HD).transpose(1, 2, 0, 3)
    grad_groups = grad_one.reshape(length, KVH, group, HD).transpose(1, 2, 0, 3)
    key_groups = keys.reshape(length, KVH, HD).transpose(1, 0, 2)
    value_groups = values.reshape(length, KVH, HD).transpose(1, 0, 2)
    places = jnp.arange(length)
    causal = places[:, None] >= places[None, :]

    def one_group(pieces):
        query_heads = pieces[0].astype(jnp.float32)
        grad_heads = pieces[1].astype(jnp.float32)
        key_head = pieces[2].astype(jnp.float32)
        value_head = pieces[3].astype(jnp.float32)
        scores = jnp.einsum('hsd,td->hst', query_heads, key_head) * head_scale
        attention = jax.nn.softmax(jnp.where(causal[None], scores, -1e+30), axis=2)
        attention_low = settle(attention)
        attended = jnp.einsum('hst,td->hsd', attention_low, value_head).astype(jnp.bfloat16)
        grad_raw = jnp.einsum('hsd,td->hst', grad_heads, value_head)
        grad_scores = attention * (grad_raw - lax.optimization_barrier(jnp.sum(attention * grad_raw, axis=2, keepdims=True)))
        grad_low = settle(grad_scores * head_scale)
        grad_query_raw = jnp.einsum('hst,td->hsd', grad_low, key_head)
        key_parts = jnp.einsum('hst,hsd->htd', grad_low, query_heads)
        value_parts = jnp.einsum('hst,hsd->htd', attention_low, grad_heads)
        key_sum = lax.optimization_barrier(jnp.sum(settle(key_parts.reshape(blocks, per_device, length, HD).sum(axis=1)), axis=0))
        value_sum = lax.optimization_barrier(jnp.sum(settle(value_parts.reshape(blocks, per_device, length, HD).sum(axis=1)), axis=0))
        return (attended, grad_query_raw, key_sum, value_sum)
    attended_g, query_g, key_g, value_g = lax.map(one_group, (query_groups, grad_groups, key_groups, value_groups))
    attended = attended_g.transpose(2, 0, 1, 3).reshape(length, HEADS * HD)
    grad_query_raw = query_g.transpose(2, 0, 1, 3).reshape(length, HEADS * HD)
    key_sums = key_g.transpose(1, 0, 2).reshape(length, KVH * HD)
    value_sums = value_g.transpose(1, 0, 2).reshape(length, KVH * HD)
    grad_key = rotate(key_sums, 0, HD, -1.0).astype(jnp.bfloat16)
    grad_value = value_sums.astype(jnp.bfloat16)
    grad_query = rotate(grad_query_raw, 0, HD, -1.0).astype(jnp.bfloat16)
    block = HEADS * HD // N_TENSOR
    key_block = KVH * HD // N_TENSOR

    def add_in(total, pieces):
        term = (jnp.dot(pieces[0], pieces[1].T, preferred_element_type=jnp.float32) + jnp.dot(pieces[2], pieces[3].T, preferred_element_type=jnp.float32) + jnp.dot(pieces[4], pieces[5].T, preferred_element_type=jnp.float32)) * in_scale
        return (total + settle(term), None)
    grad_normed, _ = lax.scan(add_in, jnp.zeros((length, width), jnp.float32), (split_columns(grad_query, block), split_columns(w_query, block), split_columns(grad_key, key_block), split_columns(w_key, key_block), split_columns(grad_value, key_block), split_columns(w_value, key_block)))
    grad_unit = grad_normed * gain
    inner = lax.optimization_barrier(jnp.mean(grad_unit * unit_rows, axis=1, keepdims=True))
    grad_tokens = (reciprocal * (grad_unit - unit_rows * inner)).astype(jnp.bfloat16)
    grad_wq = (jnp.dot(normed.T, grad_query, preferred_element_type=jnp.float32) * in_scale).astype(jnp.bfloat16)
    grad_wk = (jnp.dot(normed.T, grad_key, preferred_element_type=jnp.float32) * in_scale).astype(jnp.bfloat16)
    grad_wv = (jnp.dot(normed.T, grad_value, preferred_element_type=jnp.float32) * in_scale).astype(jnp.bfloat16)
    return (attended, grad_tokens, grad_wq, grad_wk, grad_wv)

def reference(tokens, cotangent, gain, w_query, w_key, w_value, moment_query, moment_key, moment_value):

    def single(pair):
        return sequence_pass(pair[0], pair[1], gain, w_query, w_key, w_value)
    attended, grad_tokens, stack_query, stack_key, stack_value = lax.map(single, (tokens, cotangent))
    sum_query = lax.optimization_barrier(jnp.sum(stack_query.astype(jnp.float32), axis=0))
    sum_key = lax.optimization_barrier(jnp.sum(stack_key.astype(jnp.float32), axis=0))
    sum_value = lax.optimization_barrier(jnp.sum(stack_value.astype(jnp.float32), axis=0))
    square = jnp.sum(sum_query * sum_query) + jnp.sum(sum_key * sum_key) + jnp.sum(sum_value * sum_value)
    count_all = 1.0 * D * HD * (HEADS + 2 * KVH)
    factor = lax.rsqrt(square / count_all + stat_eps)

    def advance(weight, moment, summed):
        moved = keep_rate * moment + summed * factor
        return ((weight.astype(jnp.float32) - learn_rate * moved).astype(jnp.bfloat16), moved)
    fresh_query, next_query = advance(w_query, moment_query, sum_query)
    fresh_key, next_key = advance(w_key, moment_key, sum_key)
    fresh_value, next_value = advance(w_value, moment_value, sum_value)
    return (attended, grad_tokens, fresh_query, fresh_key, fresh_value, next_query, next_key, next_value)
```

```python
import functools

import jax
import jax.numpy as jnp
from jax import lax
from jax.experimental import pallas as pl
from jax.experimental.pallas import tpu as pltpu
from jax.sharding import Mesh
from jax.sharding import PartitionSpec as P

D = 4096
HEADS = 32
KVH = 4
HD = 128
F32 = jnp.float32
BF = jnp.bfloat16
CHIPS = ("x", "yh", "yl")
TENSOR = ("x", "yh", "yl", "core")
SHARE = ("yl", "core")
DP = ("dp_0", "dp_1")
ALL = ("dp_0", "dp_1", "x", "yh", "yl", "core")

rope_base = 1000000.0
norm_eps = 1e-06
stat_eps = 1e-06
learn_rate = 0.05
keep_rate = 0.9


def rope(x, cos, sin, sign):
    lane = lax.broadcasted_iota(jnp.int32, x.shape, 1)
    nxt = pltpu.roll(x, x.shape[1]-1, 1)
    prv = pltpu.roll(x, 1, 1)
    partner = jnp.where(lane % 2 == 0, -nxt, prv)
    return x*cos + partner*(sin*sign)

NT=(((1,),(1,)),((),()))
TN=(((0,),(0,)),((),()))
def dotg(a,b,dims):
    return lax.dot_general(a,b,dims,preferred_element_type=F32)

def attn_kernel(BQ, TC, hs, q_ref, k_ref, v_ref, do_ref, cos_ref, sin_ref,
                out_ref, gq_ref, gk_ref, gv_ref, va, s_scr, r_scr, p_scr, dk, dv, m_scr, o_scr, g_scr):
    i = pl.program_id(0)
    n = pl.num_programs(0)
    T = k_ref.shape[0]
    R = 2*BQ
    @pl.when(i == 0)
    def _():
        va[:, :HD] = v_ref[...]
        va[:, HD:] = jnp.ones((T, HD), BF)
        dk[...] = jnp.zeros_like(dk)
        dv[...] = jnp.zeros_like(dv)
    q = jnp.concatenate([q_ref[:, :HD], q_ref[:, HD:]], axis=0)
    do = jnp.concatenate([do_ref[:, :HD], do_ref[:, HD:]], axis=0)
    first = i*BQ
    full = first // TC
    used = (first + BQ + TC - 1)//TC
    m_scr[...] = jnp.full((R, HD), -3e38, F32)
    def lane_max(s):
        m = m_scr[...]
        for j in range(TC//HD):
            m = jnp.maximum(m, s[:, j*HD:(j+1)*HD])
        m_scr[...] = m
    def scores(c):
        ks = k_ref[pl.ds(pl.multiple_of(c*TC, TC), TC), :]
        vs = v_ref[pl.ds(pl.multiple_of(c*TC, TC), TC), :]
        r_scr[c] = dotg(do, vs, NT)
        return dotg(q, ks, NT)
    def body1(c, _):
        s = scores(c)
        s_scr[c] = s
        lane_max(s)
        return 0
    lax.fori_loop(0, full, body1, 0)
    def body1d(c, _):
        s = scores(c)
        row = first + lax.broadcasted_iota(jnp.int32, (R, TC), 0) % BQ
        col = c*TC + lax.broadcasted_iota(jnp.int32, (R, TC), 1)
        s = jnp.where(row >= col, s, -1e30)
        s_scr[c] = s
        lane_max(s)
        return 0
    lax.fori_loop(full, used, body1d, 0)
    c2 = hs * 1.4426950408889634
    m = jnp.max(m_scr[...], axis=1, keepdims=True)
    mb = jnp.broadcast_to(m * c2, (R, HD))
    o_scr[...] = jnp.zeros_like(o_scr)
    def body2(c, _):
        s = s_scr[c]
        p = jnp.concatenate([jnp.exp2(s[:, j*HD:(j+1)*HD]*c2 - mb) for j in range(TC//HD)], axis=1).astype(BF)
        p_scr[c] = p
        o_scr[...] += jnp.dot(p, va[pl.ds(pl.multiple_of(c*TC, TC), TC), :], preferred_element_type=F32)
        return 0
    lax.fori_loop(0, used, body2, 0)
    inv = 1.0 / o_scr[:, HD:]
    o = o_scr[:, :HD] * inv
    out_ref[:, :HD] = o[:BQ].astype(BF)
    out_ref[:, HD:] = o[BQ:].astype(BF)
    dof = do.astype(F32)
    delta = jnp.broadcast_to(jnp.sum(dof*o, axis=1, keepdims=True), (R, HD))
    qn = (q.astype(F32) * (inv*hs)).astype(BF)
    don = (dof*inv).astype(BF)
    g_scr[...] = jnp.zeros_like(g_scr)
    def body3(c, _):
        at = pl.ds(pl.multiple_of(c*TC, TC), TC)
        p = p_scr[c]
        r = r_scr[c]
        pf = p.astype(F32)
        g = jnp.concatenate([pf[:, j*HD:(j+1)*HD]*(r[:, j*HD:(j+1)*HD] - delta) for j in range(TC//HD)], axis=1).astype(BF)
        g_scr[...] += jnp.dot(g, k_ref[at, :], preferred_element_type=F32)
        dk[at, :] += dotg(g, qn, TN)
        dv[at, :] += dotg(p, don, TN)
        return 0
    lax.fori_loop(0, used, body3, 0)
    gq = g_scr[...] * (inv*hs)
    here = pl.ds(pl.multiple_of(first, BQ), BQ)
    cos = cos_ref[here, :]
    sin = sin_ref[here, :]
    gq_ref[:, :HD] = rope(gq[:BQ], cos, sin, -1.0).astype(BF)
    gq_ref[:, HD:] = rope(gq[BQ:], cos, sin, -1.0).astype(BF)
    @pl.when(i == n-1)
    def _():
        gk_ref[...] = rope(dk[...], cos_ref[...], sin_ref[...], -1.0).astype(BF)
        gv_ref[...] = dv[...].astype(BF)

def attention(q, k, v, do, cos, sin, BQ=512, TC=512):
    T = q.shape[0]
    R = 2*BQ
    whole = pl.BlockSpec((T, HD), lambda i: (0, 0))
    rows = pl.BlockSpec((BQ, 2*HD), lambda i: (i, 0))
    return pl.pallas_call(
        functools.partial(attn_kernel, BQ, TC, HD**-0.5),
        grid=(T//BQ,),
        in_specs=[rows, whole, whole, rows, whole, whole],
        out_specs=[rows, rows, whole, whole],
        out_shape=[jax.ShapeDtypeStruct((T, 2*HD), BF)]*2 + [jax.ShapeDtypeStruct((T, HD), BF)]*2,
        scratch_shapes=[pltpu.VMEM((T, 2*HD), BF), pltpu.VMEM((T//TC, R, TC), F32), pltpu.VMEM((T//TC, R, TC), F32),
            pltpu.VMEM((T//TC, R, TC), BF), pltpu.VMEM((T, HD), F32), pltpu.VMEM((T, HD), F32),
            pltpu.VMEM((R, HD), F32), pltpu.VMEM((R, 2*HD), F32), pltpu.VMEM((R, HD), F32)],
        compiler_params=pltpu.CompilerParams(vmem_limit_bytes=56*1024*1024),
        name="attention",
    )(q, k, v, do, cos, sin)


def in_blocks(shard, dim, size):
    lengths = shard.shape
    pieces = shard.reshape(*lengths[:dim], size, lengths[dim] // size, *lengths[dim + 1 :])
    return jnp.moveaxis(pieces, dim, 0)


def summed_rows(shard, chips, core, dim):
    sizes = (lax.axis_size(chips), lax.axis_size(core))
    pieces = in_blocks(shard, dim, sizes[0] * sizes[1])
    inside = pieces.shape[1:]
    pieces = pieces.reshape(*sizes, *inside).swapaxes(0, 1).reshape(-1, *inside)
    pieces = lax.psum_scatter(pieces, core, scatter_dimension=0, tiled=True)
    return lax.psum_scatter(pieces, chips, scatter_dimension=0, tiled=True)[0]


def tables(length):
    within = jnp.arange(HD, dtype=jnp.int32) // 2
    rates = jnp.power(jnp.float32(rope_base), within.astype(F32) * (-2.0 / HD))
    angle = jnp.arange(length, dtype=F32)[:, None] * rates[None, :]
    return jnp.cos(angle), jnp.sin(angle)


def rotate(matrix, cos, sin):
    even = jnp.arange(matrix.shape[1]) % 2 == 0
    partner = jnp.where(even[None, :], -jnp.roll(matrix, -1, axis=1), jnp.roll(matrix, 1, axis=1))
    return matrix * cos + partner * sin


def per_device(
    tokens, cotangent, gain, w_query, w_key, w_value, moment_query, moment_key, moment_value
):
    query_width = w_query.shape[1]
    key_width = w_key.shape[1]
    width = tokens.shape[2]
    in_scale = width ** (-0.5)
    w_head = lax.all_gather(jnp.stack([w_key, w_value]), SHARE, axis=2, tiled=True)
    w_all = jnp.concatenate([w_query, w_head[0], w_head[1]], axis=1)
    inputs = tokens[0].astype(F32)
    reciprocal = lax.rsqrt(jnp.mean(inputs * inputs, axis=1, keepdims=True) + norm_eps)
    unit_rows = inputs * reciprocal
    normed = (unit_rows * gain).astype(BF)
    normed_all = lax.all_gather(normed, TENSOR, axis=0, tiled=True)
    length = normed_all.shape[0]
    cos, sin = tables(length)
    cos3, sin3 = jnp.tile(cos, (1, 3)), jnp.tile(sin, (1, 3))
    projected = jnp.dot(normed_all, w_all, preferred_element_type=F32) * in_scale
    turned = rotate(projected[:, : 3 * HD], cos3, sin3).astype(BF)
    values = projected[:, 3 * HD :].astype(BF)
    attended, grad_query, key_part, value_part = attention(
        turned[:, : 2 * HD], turned[:, 2 * HD :], values, cotangent[0], cos, sin
    )
    grads = jnp.concatenate([grad_query, key_part, value_part], axis=1)
    term = jnp.einsum("sc,dc->sd", grads, w_all, preferred_element_type=F32) * in_scale
    grad_normed = summed_rows(term.astype(BF), CHIPS, "core", 0).astype(F32)
    grad_unit = grad_normed * gain
    inner = jnp.mean(grad_unit * unit_rows, axis=1, keepdims=True)
    grad_tokens = (reciprocal * (grad_unit - unit_rows * inner)).astype(BF)[None]
    pair = lax.psum_scatter(
        jnp.stack([key_part, value_part]), SHARE, scatter_dimension=2, tiled=True
    )
    mine = jnp.concatenate([grad_query, pair[0], pair[1]], axis=1)
    grad_w = (
        jnp.einsum("sd,sc->dc", normed_all, mine, preferred_element_type=F32) * in_scale
    ).astype(BF)
    summed = lax.psum_scatter(grad_w, DP, scatter_dimension=0, tiled=True).astype(F32)
    total = lax.psum(jnp.sum(summed * summed), ALL)
    count_all = 1.0 * D * HD * (HEADS + 2 * KVH)
    factor = lax.rsqrt(total / count_all + stat_eps)
    dp_rank = lax.axis_index(DP)
    share = moment_query.shape[0]
    w_mine = jnp.concatenate([w_query, w_key, w_value], axis=1)
    own = lax.dynamic_slice_in_dim(w_mine, dp_rank * share, share, 0).astype(F32)
    moment = jnp.concatenate([moment_query, moment_key, moment_value], axis=1)
    moved = keep_rate * moment + summed * factor
    fresh = lax.all_gather((own - learn_rate * moved).astype(BF), DP, axis=0, tiled=True)
    ends = [query_width, query_width + key_width]
    fresh_query, fresh_key, fresh_value = jnp.split(fresh, ends, axis=1)
    next_query, next_key, next_value = jnp.split(moved, ends, axis=1)
    return (
        attended[None],
        grad_tokens,
        fresh_query,
        fresh_key,
        fresh_value,
        next_query,
        next_key,
        next_value,
    )


def solution(mesh):
    torus = Mesh(mesh.devices.reshape(2, 4, 2, 2, 2, 2), ALL)
    placed = (
        P(DP, TENSOR, None),
        P(DP, None, TENSOR),
        P(),
        P(None, TENSOR),
        P(None, TENSOR),
        P(None, TENSOR),
        P(DP, TENSOR),
        P(DP, TENSOR),
        P(DP, TENSOR),
    )
    return jax.shard_map(
        per_device,
        mesh=torus,
        in_specs=placed,
        out_specs=(
            P(DP, None, TENSOR),
            P(DP, TENSOR, None),
            P(None, TENSOR),
            P(None, TENSOR),
            P(None, TENSOR),
            P(DP, TENSOR),
            P(DP, TENSOR),
            P(DP, TENSOR),
        ),
        check_vma=False,
    )
```

```python
import functools

import jax
import jax.numpy as jnp
from jax import lax
from jax.experimental import pallas as pl
from jax.experimental.pallas import tpu as pltpu
from jax.sharding import Mesh
from jax.sharding import PartitionSpec as P

D = 4096
HEADS = 32
KVH = 4
HD = 128
F32 = jnp.float32
BF = jnp.bfloat16
CHIPS = ("x", "yh", "yl")
TENSOR = ("x", "yh", "yl", "core")
SHARE = ("yl", "core")
DP = ("dp_0", "dp_1")
ALL = ("dp_0", "dp_1", "x", "yh", "yl", "core")

rope_base = 1000000.0
norm_eps = 1e-06
stat_eps = 1e-06
learn_rate = 0.05
keep_rate = 0.9


def rope(x, cos, sin, sign):
    lane = lax.broadcasted_iota(jnp.int32, x.shape, 1)
    nxt = pltpu.roll(x, x.shape[1]-1, 1)
    prv = pltpu.roll(x, 1, 1)
    partner = jnp.where(lane % 2 == 0, -nxt, prv)
    return x*cos + partner*(sin*sign)

NT=(((1,),(1,)),((),()))
TN=(((0,),(0,)),((),()))
def dotg(a,b,dims):
    return lax.dot_general(a,b,dims,preferred_element_type=F32)

def attn_kernel(BQ, TC, hs, q_ref, k_ref, v_ref, do_ref, cos_ref, sin_ref,
                out_ref, gq_ref, gkv_ref, va, s_scr, r_scr, p_scr, dk, dv, m_scr, o_scr, g_scr):
    i = pl.program_id(0)
    n = pl.num_programs(0)
    T = k_ref.shape[0]
    R = 2*BQ
    @pl.when(i == 0)
    def _():
        va[:, :HD] = v_ref[...]
        va[:, HD:] = jnp.ones((T, HD), BF)
        dk[...] = jnp.zeros_like(dk)
        dv[...] = jnp.zeros_like(dv)
    q = jnp.concatenate([q_ref[:, :HD], q_ref[:, HD:]], axis=0)
    do = jnp.concatenate([do_ref[:, :HD], do_ref[:, HD:]], axis=0)
    first = i*BQ
    full = first // TC
    used = (first + BQ + TC - 1)//TC
    m_scr[...] = jnp.full((R, HD), -3e38, F32)
    def lane_max(s):
        m = m_scr[...]
        for j in range(TC//HD):
            m = jnp.maximum(m, s[:, j*HD:(j+1)*HD])
        m_scr[...] = m
    def scores(c):
        ks = k_ref[pl.ds(pl.multiple_of(c*TC, TC), TC), :]
        vs = v_ref[pl.ds(pl.multiple_of(c*TC, TC), TC), :]
        r_scr[c] = dotg(do, vs, NT)
        return dotg(q, ks, NT)
    def body1(c, _):
        s = scores(c)
        s_scr[c] = s
        lane_max(s)
        return 0
    lax.fori_loop(0, full, body1, 0)
    def body1d(c, _):
        s = scores(c)
        row = first + lax.broadcasted_iota(jnp.int32, (R, TC), 0) % BQ
        col = c*TC + lax.broadcasted_iota(jnp.int32, (R, TC), 1)
        s = jnp.where(row >= col, s, -1e30)
        s_scr[c] = s
        lane_max(s)
        return 0
    lax.fori_loop(full, used, body1d, 0)
    c2 = hs * 1.4426950408889634
    m = jnp.max(m_scr[...], axis=1, keepdims=True)
    mb = jnp.broadcast_to(m * c2, (R, HD))
    o_scr[...] = jnp.zeros_like(o_scr)
    def body2(c, _):
        s = s_scr[c]
        p = jnp.concatenate([jnp.exp2(s[:, j*HD:(j+1)*HD]*c2 - mb) for j in range(TC//HD)], axis=1).astype(BF)
        p_scr[c] = p
        o_scr[...] += jnp.dot(p, va[pl.ds(pl.multiple_of(c*TC, TC), TC), :], preferred_element_type=F32)
        return 0
    lax.fori_loop(0, used, body2, 0)
    inv = 1.0 / o_scr[:, HD:]
    o = o_scr[:, :HD] * inv
    out_ref[:, :HD] = o[:BQ].astype(BF)
    out_ref[:, HD:] = o[BQ:].astype(BF)
    dof = do.astype(F32)
    delta = jnp.broadcast_to(jnp.sum(dof*o, axis=1, keepdims=True), (R, HD))
    qn = (q.astype(F32) * (inv*hs)).astype(BF)
    don = (dof*inv).astype(BF)
    g_scr[...] = jnp.zeros_like(g_scr)
    def body3(c, _):
        at = pl.ds(pl.multiple_of(c*TC, TC), TC)
        p = p_scr[c]
        r = r_scr[c]
        pf = p.astype(F32)
        g = jnp.concatenate([pf[:, j*HD:(j+1)*HD]*(r[:, j*HD:(j+1)*HD] - delta) for j in range(TC//HD)], axis=1).astype(BF)
        g_scr[...] += jnp.dot(g, k_ref[at, :], preferred_element_type=F32)
        dk[at, :] += dotg(g, qn, TN)
        dv[at, :] += dotg(p, don, TN)
        return 0
    lax.fori_loop(0, used, body3, 0)
    gq = g_scr[...] * (inv*hs)
    here = pl.ds(pl.multiple_of(first, BQ), BQ)
    cos = cos_ref[here, :]
    sin = sin_ref[here, :]
    gq_ref[:, :HD] = rope(gq[:BQ], cos, sin, -1.0).astype(BF)
    gq_ref[:, HD:] = rope(gq[BQ:], cos, sin, -1.0).astype(BF)
    @pl.when(i == n-1)
    def _():
        gkv_ref[:, :HD] = rope(dk[...], cos_ref[...], sin_ref[...], -1.0).astype(BF)
        gkv_ref[:, HD:] = dv[...].astype(BF)

def attention(q, k, v, do, cos, sin, BQ=512, TC=512):
    T = q.shape[0]
    R = 2*BQ
    whole = pl.BlockSpec((T, HD), lambda i: (0, 0))
    rows = pl.BlockSpec((BQ, 2*HD), lambda i: (i, 0))
    return pl.pallas_call(
        functools.partial(attn_kernel, BQ, TC, HD**-0.5),
        grid=(T//BQ,),
        in_specs=[rows, whole, whole, rows, whole, whole],
        out_specs=[rows, rows, pl.BlockSpec((T, 2*HD), lambda i: (0, 0))],
        out_shape=[jax.ShapeDtypeStruct((T, 2*HD), BF)]*3,
        scratch_shapes=[pltpu.VMEM((T, 2*HD), BF), pltpu.VMEM((T//TC, R, TC), F32), pltpu.VMEM((T//TC, R, TC), F32),
            pltpu.VMEM((T//TC, R, TC), BF), pltpu.VMEM((T, HD), F32), pltpu.VMEM((T, HD), F32),
            pltpu.VMEM((R, HD), F32), pltpu.VMEM((R, 2*HD), F32), pltpu.VMEM((R, HD), F32)],
        compiler_params=pltpu.CompilerParams(vmem_limit_bytes=56*1024*1024),
        name="attention",
    )(q, k, v, do, cos, sin)


MESH_ID = pl.DeviceIdType.MESH
INNER = 4


def place():
    at = lax.axis_index
    return dict(
        xl=at("dp_0"), z=at("dp_1"), xh=at("x"), y=at("yh") * 2 + at("yl"), core=at("core")
    )


def device(**moved):
    names = {}
    for key, value in moved.items():
        if key == "y":
            names["yh"] = value // 2
            names["yl"] = value % 2
        elif key == "x":
            names["x"] = value // 2
            names["dp_0"] = value % 2
        else:
            names[{"xl": "dp_0", "z": "dp_1", "xh": "x", "core": "core"}[key]] = value
    return names


class Link:
    def __init__(self, send, recv):
        self.send, self.recv, self.used, self.sent = send, recv, 0, []

    def slot(self):
        self.used += 1
        return self.used - 1

    def start(self, slot, src, dst, to):
        copy = pltpu.make_async_remote_copy(
            src_ref=src,
            dst_ref=dst,
            send_sem=self.send.at[slot],
            recv_sem=self.recv.at[slot],
            device_id=to,
            device_id_type=MESH_ID,
        )
        copy.start()
        self.sent.append(copy)

    def wait(self, slot, landed, to):
        pltpu.make_async_remote_copy(
            src_ref=landed,
            dst_ref=landed,
            send_sem=self.send.at[slot],
            recv_sem=self.recv.at[slot],
            device_id=to,
            device_id_type=MESH_ID,
        ).wait_recv()

    def drain(self):
        for copy in self.sent:
            copy.wait_send()


def added(ref, other):
    ref[...] = (ref[...].astype(F32) + other[...].astype(F32)).astype(BF)


def ring_reduce(link, me, up, down, piece, half, part_low, part_high, full_low, full_high):
    s = [link.slot() for _ in range(4)]
    far = piece(lax.rem(me + 2, 4))
    link.start(s[0], half(far, 0), part_low, up)
    link.start(s[1], half(far, 1), part_high, down)
    yield
    above = piece(lax.rem(me + 1, 4))
    link.wait(s[0], part_low, down)
    added(half(above, 0), part_low)
    link.start(s[2], above, full_low, up)
    below = piece(lax.rem(me + 3, 4))
    link.wait(s[1], part_high, up)
    added(half(below, 1), part_high)
    link.start(s[3], below, full_high, down)
    yield
    link.wait(s[2], full_low, down)
    link.wait(s[3], full_high, up)


def ring_spread(link, me, up, down, piece, half):
    s = [link.slot() for _ in range(4)]
    mine = piece(me)
    link.start(s[0], mine, mine, up)
    link.start(s[1], mine, mine, down)
    yield
    low, high = piece(lax.rem(me + 3, 4)), piece(lax.rem(me + 1, 4))
    link.wait(s[0], low, down)
    link.start(s[2], half(low, 0), half(low, 0), up)
    link.wait(s[1], high, up)
    link.start(s[3], half(high, 1), half(high, 1), down)
    yield
    far = piece(lax.rem(me + 2, 4))
    link.wait(s[2], half(far, 0), down)
    link.wait(s[3], half(far, 1), up)


def finish(steps):
    for _ in steps:
        pass


def greet(others):
    barrier = pltpu.get_barrier_semaphore()
    for other in others:
        pl.semaphore_signal(barrier, inc=1, device_id=other, device_id_type=MESH_ID)
    pl.semaphore_wait(barrier, len(others))


def rows_part(first, count):
    return lambda ref, part: ref.at[pl.ds(first if part == 0 else first + count[0], count[part])]


LOW = 64


def rows_chain(r, link, p):
    core, y, xh = p["core"], p["y"], p["xh"]
    sib, across = device(core=1 - core), device(xh=1 - xh)
    up, down = device(y=lax.rem(y + 1, 4)), device(y=lax.rem(y + 3, 4))
    near = y + 1 - 2 * lax.rem(y, 2)
    pair = device(y=near)
    gq, gkv, sib_q, sib_kv, cat = r["gq"], r["gkv"], r["sib_q"], r["sib_kv"], r["cat"]
    one, two = link.slot(), link.slot()
    link.start(one, gkv.at[:, 1 - core], sib_kv, sib)
    link.start(two, gq.at[:, 1 - core], sib_q, sib)
    yield
    link.wait(one, sib_kv, sib)
    added(sib_kv, gkv.at[:, core])
    three = link.slot()
    link.start(three, sib_kv, r["pair_kv"], pair)
    link.wait(two, sib_q, sib)
    cat[:, :, : 2 * HD] = gq[:, core]
    cat[:, :, 2 * HD : 4 * HD] = sib_q[...]
    cat[:, :, 4 * HD :] = sib_kv[...]
    rows = 4 * cat.shape[1]
    width = r["part"].shape[3]
    step = 512
    scale = width ** (-0.5)

    def products(side):
        left = cat[pl.ds(side * 4, 4)].reshape(rows, 6 * HD)

        def body(c, _):
            at = pl.ds(pl.multiple_of(c * step, step), step)
            out = dotg(left, r["w3"][at, :], NT) * scale
            r["part"][side, :, :, at] = out.astype(BF).reshape(4, rows // 4, step)
            return 0

        lax.fori_loop(0, width // step, body, 0)

    part = r["part"]
    high = part.shape[2] - LOW
    top, rest = pl.ds(0, LOW), pl.ds(LOW, high)
    cut = lambda n: (lambda ref, i: ref.at[pl.ds(0 if i == 0 else n // 2, n // 2)])

    def ring(side, rows_at, n, bufs):
        return ring_reduce(
            link, y, up, down, lambda q: part.at[side, q, rows_at], cut(n), *bufs
        )

    def bufs(k):
        return tuple(r[name].at[k] for name in ("part_low", "part_high", "full_low", "full_high"))

    products(1 - xh)
    across_slots = [link.slot() for _ in range(4)]
    for q in range(4):
        link.start(across_slots[q], part.at[1 - xh, q, rest], r["cross"].at[q], across)
    far_ring = ring(1 - xh, top, LOW, bufs(0))
    next(far_ring)
    products(xh)
    near_ring = ring(xh, top, LOW, bufs(1))
    next(near_ring)
    yield
    link.wait(three, r["pair_kv"], pair)
    total = (sib_kv[...].astype(F32) + r["pair_kv"][...].astype(F32)).astype(BF)
    r["kv_all"][:, core] = total
    four = link.slot()
    link.start(four, r["kv_all"].at[:, core], r["kv_all"].at[:, core], sib)
    next(far_ring)
    link.wait(four, r["kv_all"].at[:, 1 - core], sib)
    yield
    next(near_ring)
    yield
    finish(far_ring)
    k = 0
    done = part.at[1 - xh, y, top]
    done[...] = (
        done[...].astype(F32)
        + r["full_low"][k].astype(F32)
        + r["full_high"][k].astype(F32)
    ).astype(BF)
    last = link.slot()
    link.start(last, done, r["cross_top"], across)
    yield
    for q in range(4):
        link.wait(across_slots[q], r["cross"].at[q], across)
        added(part.at[xh, q, rest], r["cross"].at[q])
    rest_ring = ring(xh, rest, high, bufs(2))
    next(rest_ring)
    yield
    finish(near_ring)
    next(rest_ring)
    yield
    finish(rest_ring)
    link.wait(last, r["cross_top"], across)
    own = part.at[xh, y]
    top_rows = (
        own[top].astype(F32)
        + r["full_low"][1].astype(F32)
        + r["full_high"][1].astype(F32)
        + r["cross_top"][...].astype(F32)
    )
    rest_rows = (
        own[rest].astype(F32) + r["full_low"][2].astype(F32) + r["full_high"][2].astype(F32)
    )
    for first, grad_normed in ((0, top_rows), (LOW, rest_rows)):
        at = pl.ds(first, grad_normed.shape[0])
        inputs = r["tokens"][at, :].astype(F32)
        reciprocal = lax.rsqrt(jnp.mean(inputs * inputs, axis=1, keepdims=True) + norm_eps)
        unit = inputs * reciprocal
        grad_unit = grad_normed * r["gain"][...]
        inner = jnp.mean(grad_unit * unit, axis=1, keepdims=True)
        r["grad_tokens"][at, :] = (reciprocal * (grad_unit - unit * inner)).astype(BF)


def weight_chain(r, link, p):
    core, y, xh, xl, z = p["core"], p["y"], p["xh"], p["xl"], p["z"]
    up, down = device(z=lax.rem(z + 1, 4)), device(z=lax.rem(z + 3, 4))
    beside = device(xl=1 - xl)
    wide = 2 * HD
    thin = HD // INNER
    length = r["turned"].shape[1]
    width = r["rows"].shape[0] * r["rows"].shape[2]
    scale = width ** (-0.5)
    which = pl.multiple_of((lax.rem(y, 2) * 2 + core) * thin, thin)
    r["turned"][:wide, :] = r["gq"][...].reshape(length, wide).T
    r["kv_turned"][...] = r["kv_all"][...].reshape(length, wide).T
    r["turned"][wide : wide + thin, :] = r["kv_turned"][pl.ds(which, thin), :]
    r["turned"][wide + thin :, :] = r["kv_turned"][pl.ds(which + HD, thin), :]
    grad = r["grad"]

    def body(c, _):
        r["arrive"](c)
        out = jnp.dot(r["turned"][...], r["rows"][c], preferred_element_type=F32) * scale
        grad[c % 4, c // 4] = out.astype(BF)
        return 0

    lax.fori_loop(0, 8, body, 0)
    index = lambda ref, i: ref.at[i]
    ring = ring_reduce(
        link, z, up, down, lambda q: grad.at[q], index, r["z_low"], r["z_high"], r["z_full_low"], r["z_full_high"]
    )
    next(ring)
    yield
    next(ring)
    yield
    finish(ring)
    mine = grad.at[z]
    mine[...] = (
        mine[...].astype(F32) + r["z_full_low"][...].astype(F32) + r["z_full_high"][...].astype(F32)
    ).astype(BF)
    s = link.slot()
    link.start(s, mine.at[1 - xl], r["beside"], beside)
    yield
    link.wait(s, r["beside"], beside)
    summed = mine[xl].astype(F32) + r["beside"][...].astype(F32)
    r["summed"][...] = summed
    square = jnp.sum(summed * summed, axis=0, keepdims=True)
    square = jnp.sum(square, axis=1, keepdims=True)
    x = xh * 2 + xl
    stages = (
        [device(core=1 - core)],
        [device(x=lax.rem(x + i, 4)) for i in (1, 2, 3)],
        [device(y=lax.rem(y + i, 4)) for i in (1, 2, 3)],
        [device(z=lax.rem(z + i, 4)) for i in (1, 2, 3)],
    )
    total = jnp.broadcast_to(square, (8, HD))
    for k, others in enumerate(stages):
        r["square"][k] = total
        slots = [link.slot() for _ in others]
        for i, other in enumerate(others):
            link.start(slots[i], r["square"].at[k], r["squares"].at[k, i], other)
        yield
        for i, other in enumerate(others):
            back = others[len(others) - 1 - i]
            link.wait(slots[i], r["squares"].at[k, i], back)
            total = total + r["squares"][k, i]
    count_all = 1.0 * D * HD * (HEADS + 2 * KVH)
    factor = lax.rsqrt(total[:1, :1] / count_all + stat_eps)
    moved = keep_rate * r["moment"][...] + r["summed"][...] * factor
    r["next"][...] = moved
    fresh = r["fresh"]
    fresh[z, xl] = (r["own"][...].astype(F32) - learn_rate * moved).astype(BF)
    s = link.slot()
    link.start(s, fresh.at[z, xl], fresh.at[z, xl], beside)
    n = r["own"].shape[0] // 2
    cut = lambda ref, i: ref.at[pl.ds(i * n, n)]
    first = ring_spread(link, z, up, down, lambda q: fresh.at[q, xl], cut)
    next(first)
    yield
    link.wait(s, fresh.at[z, 1 - xl], beside)
    second = ring_spread(link, z, up, down, lambda q: fresh.at[q, 1 - xl], cut)
    next(second)
    next(first)
    yield
    finish(first)
    next(second)
    yield
    finish(second)


ROW_NAMES = ("gq", "gkv", "w3", "tokens", "gain", "rows_hbm", "moment", "own")
OUT_NAMES = ("grad_tokens", "fresh", "next")


def back_kernel(names, *refs):
    r = dict(zip(names, refs))
    p = place()
    link = Link(r["send"], r["recv"])
    copies = []
    step = r["rows"].shape[2]
    for c in range(8):
        copy = pltpu.make_async_copy(
            r["rows_hbm"].at[:, pl.ds(c * step, step)], r["rows"].at[c], r["load"].at[c]
        )
        copy.start()

    def arrive(c):
        pltpu.make_async_copy(
            r["rows_hbm"].at[:, pl.ds(pl.multiple_of(c * step, step), step)], r["rows"].at[c], r["load"].at[c]
        ).wait()

    r["arrive"] = arrive
    x = p["xh"] * 2 + p["xl"]
    others = [device(core=1 - p["core"])]
    for i in (1, 2, 3):
        others.append(device(x=lax.rem(x + i, 4)))
        others.append(device(y=lax.rem(p["y"] + i, 4)))
        others.append(device(z=lax.rem(p["z"] + i, 4)))
    greet(others)
    rows, weights = rows_chain(r, link, p), weight_chain(r, link, p)
    for which in ORDER:
        next(rows if which == "r" else weights, None)
    finish(rows)
    finish(weights)
    link.drain()


ORDER = "rrrr" + "wrwrwrwrwrw"


def back(gq, gkv, w3, tokens, gain, rows, moment, own):
    length, width = rows.shape
    columns, share = own.shape
    block = length // 16
    halves = (block - LOW, LOW)
    v = pltpu.VMEM
    scratch = dict(
        sib_q=v((8, block, 2 * HD), BF),
        sib_kv=v((8, block, 2 * HD), BF),
        pair_kv=v((8, block, 2 * HD), BF),
        kv_all=v((8, 2, block, 2 * HD), BF),
        cat=v((8, block, 6 * HD), BF),
        part=v((2, 4, block, width), BF),
        part_low=v((3, LOW // 2, width), BF),
        part_high=v((3, LOW // 2, width), BF),
        full_low=v((3, LOW, width), BF),
        full_high=v((3, LOW, width), BF),
        cross=v((4, block - LOW, width), BF),
        cross_top=v((LOW, width), BF),
        rows=v((8, length, width // 8), BF),
        load=pltpu.SemaphoreType.DMA((8,)),
        turned=v((columns, length), BF),
        kv_turned=v((2 * HD, length), BF),
        grad=v((4, 2, columns, share), BF),
        z_low=v((columns, share), BF),
        z_high=v((columns, share), BF),
        z_full_low=v((2, columns, share), BF),
        z_full_high=v((2, columns, share), BF),
        beside=v((columns, share), BF),
        summed=v((columns, share), F32),
        square=v((4, 8, HD), F32),
        squares=v((4, 3, 8, HD), F32),
        send=pltpu.SemaphoreType.DMA((48,)),
        recv=pltpu.SemaphoreType.DMA((48,)),
    )
    whole = pl.BlockSpec(memory_space=pltpu.VMEM)
    names = ROW_NAMES + OUT_NAMES + tuple(scratch)
    return pl.pallas_call(
        functools.partial(back_kernel, names),
        in_specs=[pl.BlockSpec(memory_space=pl.ANY) if n == "rows_hbm" else whole for n in ROW_NAMES],
        out_specs=[whole] * 3,
        out_shape=[
            jax.ShapeDtypeStruct((block, width), BF),
            jax.ShapeDtypeStruct((4, 2, columns, share), BF),
            jax.ShapeDtypeStruct((columns, share), F32),
        ],
        scratch_shapes=list(scratch.values()),
        compiler_params=pltpu.CompilerParams(
            collective_id=1, has_side_effects=True, vmem_limit_bytes=62 * 1024 * 1024
        ),
        name="back",
    )(gq, gkv, w3, tokens, gain, rows, moment, own)


def tables(length):
    within = jnp.arange(HD, dtype=jnp.int32) // 2
    rates = jnp.power(jnp.float32(rope_base), within.astype(F32) * (-2.0 / HD))
    angle = jnp.arange(length, dtype=F32)[:, None] * rates[None, :]
    return jnp.cos(angle), jnp.sin(angle)


def rotate(matrix, cos, sin):
    even = jnp.arange(matrix.shape[1]) % 2 == 0
    partner = jnp.where(even[None, :], -jnp.roll(matrix, -1, axis=1), jnp.roll(matrix, 1, axis=1))
    return matrix * cos + partner * sin


def per_device(
    tokens, cotangent, gain, w_query, w_key, w_value, moment_query, moment_key, moment_value
):
    query_width = w_query.shape[1]
    key_width = w_key.shape[1]
    width = tokens.shape[2]
    in_scale = width ** (-0.5)
    w_head = lax.all_gather(jnp.stack([w_key, w_value]), SHARE, axis=2, tiled=True)
    w_other = lax.ppermute(w_query, "core", [(0, 1), (1, 0)])
    w3 = jnp.concatenate([w_query, w_other, w_head[0], w_head[1]], axis=1)
    w_all = jnp.concatenate([w_query, w_head[0], w_head[1]], axis=1)
    inputs = tokens[0].astype(F32)
    reciprocal = lax.rsqrt(jnp.mean(inputs * inputs, axis=1, keepdims=True) + norm_eps)
    unit_rows = inputs * reciprocal
    normed = (unit_rows * gain).astype(BF)
    normed_all = lax.all_gather(normed, TENSOR, axis=0, tiled=True)
    length = normed_all.shape[0]
    cos, sin = tables(length)
    cos3, sin3 = jnp.tile(cos, (1, 3)), jnp.tile(sin, (1, 3))
    projected = jnp.dot(normed_all, w_all, preferred_element_type=F32) * in_scale
    turned = rotate(projected[:, : 3 * HD], cos3, sin3).astype(BF)
    values = projected[:, 3 * HD :].astype(BF)
    attended, grad_query, grad_kv = attention(
        turned[:, : 2 * HD], turned[:, 2 * HD :], values, cotangent[0], cos, sin
    )
    dp_rank = lax.axis_index(DP)
    share = moment_query.shape[0]
    w_mine = jnp.concatenate([w_query, w_key, w_value], axis=1)
    own = lax.dynamic_slice_in_dim(w_mine, dp_rank * share, share, 0).T
    moment = jnp.concatenate([moment_query, moment_key, moment_value], axis=1).T
    by_block = (8, 2, length // 16, 2 * HD)
    grad_tokens, fresh, moved = back(
        grad_query.reshape(by_block),
        grad_kv.reshape(by_block),
        w3,
        tokens[0],
        gain[None],
        normed_all,
        moment,
        own,
    )
    moved = moved.T
    fresh = fresh.transpose(1, 0, 3, 2).reshape(width, -1)
    ends = [query_width, query_width + key_width]
    fresh_query, fresh_key, fresh_value = jnp.split(fresh, ends, axis=1)
    next_query, next_key, next_value = jnp.split(moved, ends, axis=1)
    return (
        attended[None],
        grad_tokens[None],
        fresh_query,
        fresh_key,
        fresh_value,
        next_query,
        next_key,
        next_value,
    )


def solution(mesh):
    torus = Mesh(mesh.devices.reshape(2, 4, 2, 2, 2, 2), ALL)
    placed = (
        P(DP, TENSOR, None),
        P(DP, None, TENSOR),
        P(),
        P(None, TENSOR),
        P(None, TENSOR),
        P(None, TENSOR),
        P(DP, TENSOR),
        P(DP, TENSOR),
        P(DP, TENSOR),
    )
    return jax.shard_map(
        per_device,
        mesh=torus,
        in_specs=placed,
        out_specs=(
            P(DP, None, TENSOR),
            P(DP, TENSOR, None),
            P(None, TENSOR),
            P(None, TENSOR),
            P(None, TENSOR),
            P(DP, TENSOR),
            P(DP, TENSOR),
            P(DP, TENSOR),
        ),
        check_vma=False,
    )
```

```python
import functools

import jax
import jax.numpy as jnp
import numpy as np
from jax import lax
from jax.experimental import pallas as pl
from jax.experimental.pallas import tpu as pltpu
from jax.sharding import Mesh
from jax.sharding import PartitionSpec as P

D = 4096
HEADS = 32
KVH = 4
HD = 128
F32 = jnp.float32
BF = jnp.bfloat16
CHIPS = ("x", "yh", "yl")
TENSOR = ("x", "yh", "yl", "core")
SHARE = ("yl", "core")
DP = ("dp_0", "dp_1")
ALL = ("dp_0", "dp_1", "x", "yh", "yl", "core")

rope_base = 1000000.0
norm_eps = 1e-06
stat_eps = 1e-06
learn_rate = 0.05
keep_rate = 0.9


def rope(x, cos, sin, sign):
    lane = lax.broadcasted_iota(jnp.int32, x.shape, 1)
    nxt = pltpu.roll(x, x.shape[1]-1, 1)
    prv = pltpu.roll(x, 1, 1)
    partner = jnp.where(lane % 2 == 0, -nxt, prv)
    return x*cos + partner*(sin*sign)

NT=(((1,),(1,)),((),()))
TN=(((0,),(0,)),((),()))
def dotg(a,b,dims):
    return lax.dot_general(a,b,dims,preferred_element_type=F32)

def attn_kernel(BQ, TC, hs, q_ref, k_ref, v_ref, do_ref, cos_ref, sin_ref,
                out_ref, gq_ref, gkv_ref, va, s_scr, r_scr, p_scr, dk, dv, m_scr, o_scr, g_scr):
    i = pl.program_id(0)
    n = pl.num_programs(0)
    T = k_ref.shape[0]
    R = 2*BQ
    @pl.when(i == 0)
    def _():
        va[:, :HD] = v_ref[...]
        va[:, HD:] = jnp.ones((T, HD), BF)
        dk[...] = jnp.zeros_like(dk)
        dv[...] = jnp.zeros_like(dv)
    q = jnp.concatenate([q_ref[:, :HD], q_ref[:, HD:]], axis=0)
    do = jnp.concatenate([do_ref[:, :HD], do_ref[:, HD:]], axis=0)
    first = i*BQ
    full = first // TC
    used = (first + BQ + TC - 1)//TC
    m_scr[...] = jnp.full((R, HD), -3e38, F32)
    def lane_max(s):
        m = m_scr[...]
        for j in range(TC//HD):
            m = jnp.maximum(m, s[:, j*HD:(j+1)*HD])
        m_scr[...] = m
    def scores(c):
        ks = k_ref[pl.ds(pl.multiple_of(c*TC, TC), TC), :]
        vs = v_ref[pl.ds(pl.multiple_of(c*TC, TC), TC), :]
        r_scr[c] = dotg(do, vs, NT)
        return dotg(q, ks, NT)
    def body1(c, _):
        s = scores(c)
        s_scr[c] = s
        lane_max(s)
        return 0
    lax.fori_loop(0, full, body1, 0)
    def body1d(c, _):
        s = scores(c)
        row = first + lax.broadcasted_iota(jnp.int32, (R, TC), 0) % BQ
        col = c*TC + lax.broadcasted_iota(jnp.int32, (R, TC), 1)
        s = jnp.where(row >= col, s, -1e30)
        s_scr[c] = s
        lane_max(s)
        return 0
    lax.fori_loop(full, used, body1d, 0)
    c2 = hs * 1.4426950408889634
    m = jnp.max(m_scr[...], axis=1, keepdims=True)
    mb = jnp.broadcast_to(m * c2, (R, HD))
    o_scr[...] = jnp.zeros_like(o_scr)
    def body2(c, _):
        s = s_scr[c]
        p = jnp.concatenate([jnp.exp2(s[:, j*HD:(j+1)*HD]*c2 - mb) for j in range(TC//HD)], axis=1).astype(BF)
        p_scr[c] = p
        o_scr[...] += jnp.dot(p, va[pl.ds(pl.multiple_of(c*TC, TC), TC), :], preferred_element_type=F32)
        return 0
    lax.fori_loop(0, used, body2, 0)
    inv = 1.0 / o_scr[:, HD:]
    o = o_scr[:, :HD] * inv
    out_ref[:, :HD] = o[:BQ].astype(BF)
    out_ref[:, HD:] = o[BQ:].astype(BF)
    dof = do.astype(F32)
    delta = jnp.broadcast_to(jnp.sum(dof*o, axis=1, keepdims=True), (R, HD))
    qn = (q.astype(F32) * (inv*hs)).astype(BF)
    don = (dof*inv).astype(BF)
    g_scr[...] = jnp.zeros_like(g_scr)
    def body3(c, _):
        at = pl.ds(pl.multiple_of(c*TC, TC), TC)
        p = p_scr[c]
        r = r_scr[c]
        pf = p.astype(F32)
        g = jnp.concatenate([pf[:, j*HD:(j+1)*HD]*(r[:, j*HD:(j+1)*HD] - delta) for j in range(TC//HD)], axis=1).astype(BF)
        g_scr[...] += jnp.dot(g, k_ref[at, :], preferred_element_type=F32)
        dk[at, :] += dotg(g, qn, TN)
        dv[at, :] += dotg(p, don, TN)
        return 0
    lax.fori_loop(0, used, body3, 0)
    gq = g_scr[...] * (inv*hs)
    here = pl.ds(pl.multiple_of(first, BQ), BQ)
    cos = cos_ref[here, :]
    sin = sin_ref[here, :]
    gq_ref[:, :HD] = rope(gq[:BQ], cos, sin, -1.0).astype(BF)
    gq_ref[:, HD:] = rope(gq[BQ:], cos, sin, -1.0).astype(BF)
    @pl.when(i == n-1)
    def _():
        gkv_ref[:, :HD] = rope(dk[...], cos_ref[...], sin_ref[...], -1.0).astype(BF)
        gkv_ref[:, HD:] = dv[...].astype(BF)

def attention(q, k, v, do, cos, sin, BQ=512, TC=512):
    T = q.shape[0]
    R = 2*BQ
    whole = pl.BlockSpec((T, HD), lambda i: (0, 0))
    rows = pl.BlockSpec((BQ, 2*HD), lambda i: (i, 0))
    return pl.pallas_call(
        functools.partial(attn_kernel, BQ, TC, HD**-0.5),
        grid=(T//BQ,),
        in_specs=[rows, whole, whole, rows, whole, whole],
        out_specs=[rows, rows, pl.BlockSpec((T, 2*HD), lambda i: (0, 0))],
        out_shape=[jax.ShapeDtypeStruct((T, 2*HD), BF)]*3,
        scratch_shapes=[pltpu.VMEM((T, 2*HD), BF), pltpu.VMEM((T//TC, R, TC), F32), pltpu.VMEM((T//TC, R, TC), F32),
            pltpu.VMEM((T//TC, R, TC), BF), pltpu.VMEM((T, HD), F32), pltpu.VMEM((T, HD), F32),
            pltpu.VMEM((R, HD), F32), pltpu.VMEM((R, 2*HD), F32), pltpu.VMEM((R, HD), F32)],
        compiler_params=pltpu.CompilerParams(vmem_limit_bytes=56*1024*1024),
        name="attention",
    )(q, k, v, do, cos, sin)


MESH_ID = pl.DeviceIdType.MESH
INNER = 4


def place():
    at = lax.axis_index
    return dict(
        xl=at("dp_0"), z=at("dp_1"), xh=at("x"), y=at("yh") * 2 + at("yl"), core=at("core")
    )


def device(**moved):
    names = {}
    for key, value in moved.items():
        if key == "y":
            names["yh"] = value // 2
            names["yl"] = value % 2
        elif key == "x":
            names["x"] = value // 2
            names["dp_0"] = value % 2
        else:
            names[{"xl": "dp_0", "z": "dp_1", "xh": "x", "core": "core"}[key]] = value
    return names


class Link:
    def __init__(self, send, recv):
        self.send, self.recv, self.used, self.sent = send, recv, 0, []

    def slot(self):
        self.used += 1
        return self.used - 1

    def start(self, slot, src, dst, to):
        copy = pltpu.make_async_remote_copy(
            src_ref=src,
            dst_ref=dst,
            send_sem=self.send.at[slot],
            recv_sem=self.recv.at[slot],
            device_id=to,
            device_id_type=MESH_ID,
        )
        copy.start()
        self.sent.append(copy)

    def wait(self, slot, landed, to):
        pltpu.make_async_remote_copy(
            src_ref=landed,
            dst_ref=landed,
            send_sem=self.send.at[slot],
            recv_sem=self.recv.at[slot],
            device_id=to,
            device_id_type=MESH_ID,
        ).wait_recv()

    def drain(self):
        for copy in self.sent:
            copy.wait_send()


def added(ref, other):
    ref[...] = (ref[...].astype(F32) + other[...].astype(F32)).astype(BF)


def ring_reduce(link, me, up, down, piece, half, part_low, part_high, full_low, full_high):
    s = [link.slot() for _ in range(4)]
    far = piece(lax.rem(me + 2, 4))
    link.start(s[0], half(far, 0), part_low, up)
    link.start(s[1], half(far, 1), part_high, down)
    yield
    above = piece(lax.rem(me + 1, 4))
    link.wait(s[0], part_low, down)
    added(half(above, 0), part_low)
    link.start(s[2], above, full_low, up)
    below = piece(lax.rem(me + 3, 4))
    link.wait(s[1], part_high, up)
    added(half(below, 1), part_high)
    link.start(s[3], below, full_high, down)
    yield
    link.wait(s[2], full_low, down)
    link.wait(s[3], full_high, up)


def ring_spread(link, me, up, down, piece, half):
    s = [link.slot() for _ in range(4)]
    mine = piece(me)
    link.start(s[0], mine, mine, up)
    link.start(s[1], mine, mine, down)
    yield
    low, high = piece(lax.rem(me + 3, 4)), piece(lax.rem(me + 1, 4))
    link.wait(s[0], low, down)
    link.start(s[2], half(low, 0), half(low, 0), up)
    link.wait(s[1], high, up)
    link.start(s[3], half(high, 1), half(high, 1), down)
    yield
    far = piece(lax.rem(me + 2, 4))
    link.wait(s[2], half(far, 0), down)
    link.wait(s[3], half(far, 1), up)


def finish(steps):
    for _ in steps:
        pass


def greet(others):
    barrier = pltpu.get_barrier_semaphore()
    for other in others:
        pl.semaphore_signal(barrier, inc=1, device_id=other, device_id_type=MESH_ID)
    pl.semaphore_wait(barrier, len(others))


def rows_part(first, count):
    return lambda ref, part: ref.at[pl.ds(first if part == 0 else first + count[0], count[part])]


LOW = 64


def rows_chain(r, link, p):
    core, y, xh = p["core"], p["y"], p["xh"]
    sib, across = device(core=1 - core), device(xh=1 - xh)
    up, down = device(y=lax.rem(y + 1, 4)), device(y=lax.rem(y + 3, 4))
    near = y + 1 - 2 * lax.rem(y, 2)
    pair = device(y=near)
    gq, gkv, sib_q, sib_kv, cat = r["gq"], r["gkv"], r["sib_q"], r["sib_kv"], r["cat"]
    one, two = link.slot(), link.slot()
    link.start(one, gkv.at[:, 1 - core], sib_kv, sib)
    link.start(two, gq.at[:, 1 - core], sib_q, sib)
    yield
    link.wait(one, sib_kv, sib)
    added(sib_kv, gkv.at[:, core])
    three = link.slot()
    link.start(three, sib_kv, r["pair_kv"], pair)
    link.wait(two, sib_q, sib)
    cat[:, :, : 2 * HD] = gq[:, core]
    cat[:, :, 2 * HD : 4 * HD] = sib_q[...]
    cat[:, :, 4 * HD :] = sib_kv[...]
    rows = 4 * cat.shape[1]
    width = r["part"].shape[3]
    step = 512
    scale = width ** (-0.5)

    def products(side):
        left = cat[pl.ds(side * 4, 4)].reshape(rows, 6 * HD)

        def body(c, _):
            at = pl.ds(pl.multiple_of(c * step, step), step)
            out = dotg(left[:, : 2 * HD], r["w_query"][at, :], NT)
            out = out + dotg(left[:, 2 * HD : 4 * HD], r["w_other"][at, :], NT)
            out = out + jnp.dot(left[:, 4 * HD :], r["w_head"][:, at], preferred_element_type=F32)
            out = out * scale
            r["part"][side, :, :, at] = out.astype(BF).reshape(4, rows // 4, step)
            return 0

        lax.fori_loop(0, width // step, body, 0)

    part = r["part"]
    high = part.shape[2] - LOW
    top, rest = pl.ds(0, LOW), pl.ds(LOW, high)
    cut = lambda n: (lambda ref, i: ref.at[pl.ds(0 if i == 0 else n // 2, n // 2)])

    def ring(side, rows_at, n, bufs):
        return ring_reduce(
            link, y, up, down, lambda q: part.at[side, q, rows_at], cut(n), *bufs
        )

    def bufs(k):
        return tuple(r[name].at[k] for name in ("part_low", "part_high", "full_low", "full_high"))

    products(1 - xh)
    across_slots = [link.slot() for _ in range(4)]
    for q in range(4):
        link.start(across_slots[q], part.at[1 - xh, q, rest], r["cross"].at[q], across)
    far_ring = ring(1 - xh, top, LOW, bufs(0))
    next(far_ring)
    products(xh)
    near_ring = ring(xh, top, LOW, bufs(1))
    next(near_ring)
    yield
    link.wait(three, r["pair_kv"], pair)
    total = (sib_kv[...].astype(F32) + r["pair_kv"][...].astype(F32)).astype(BF)
    r["kv_all"][:, core] = total
    four = link.slot()
    link.start(four, r["kv_all"].at[:, core], r["kv_all"].at[:, core], sib)
    next(far_ring)
    link.wait(four, r["kv_all"].at[:, 1 - core], sib)
    yield
    next(near_ring)
    yield
    finish(far_ring)
    k = 0
    done = part.at[1 - xh, y, top]
    done[...] = (
        done[...].astype(F32)
        + r["full_low"][k].astype(F32)
        + r["full_high"][k].astype(F32)
    ).astype(BF)
    last = link.slot()
    link.start(last, done, r["cross_top"], across)
    yield
    for q in range(4):
        link.wait(across_slots[q], r["cross"].at[q], across)
        added(part.at[xh, q, rest], r["cross"].at[q])
    rest_ring = ring(xh, rest, high, bufs(2))
    next(rest_ring)
    yield
    finish(near_ring)
    next(rest_ring)
    yield
    finish(rest_ring)
    link.wait(last, r["cross_top"], across)
    own = part.at[xh, y]
    top_rows = (
        own[top].astype(F32)
        + r["full_low"][1].astype(F32)
        + r["full_high"][1].astype(F32)
        + r["cross_top"][...].astype(F32)
    )
    rest_rows = (
        own[rest].astype(F32) + r["full_low"][2].astype(F32) + r["full_high"][2].astype(F32)
    )
    for first, grad_normed in ((0, top_rows), (LOW, rest_rows)):
        at = pl.ds(first, grad_normed.shape[0])
        inputs = r["tokens"][at, :].astype(F32)
        reciprocal = lax.rsqrt(jnp.mean(inputs * inputs, axis=1, keepdims=True) + norm_eps)
        unit = inputs * reciprocal
        grad_unit = grad_normed * r["gain"][...]
        inner = jnp.mean(grad_unit * unit, axis=1, keepdims=True)
        r["grad_tokens"][at, :] = (reciprocal * (grad_unit - unit * inner)).astype(BF)


def weight_chain(r, link, p):
    core, y, xh, xl, z = p["core"], p["y"], p["xh"], p["xl"], p["z"]
    up, down = device(z=lax.rem(z + 1, 4)), device(z=lax.rem(z + 3, 4))
    beside = device(xl=1 - xl)
    wide = 2 * HD
    thin = HD // INNER
    length = r["turned"].shape[1]
    width = r["rows"].shape[0] * r["rows"].shape[2]
    scale = width ** (-0.5)
    which = pl.multiple_of((lax.rem(y, 2) * 2 + core) * thin, thin)
    r["turned"][:wide, :] = r["gq"][...].reshape(length, wide).T
    r["kv_turned"][...] = r["kv_all"][...].reshape(length, wide).T
    r["turned"][wide : wide + thin, :] = r["kv_turned"][pl.ds(which, thin), :]
    r["turned"][wide + thin :, :] = r["kv_turned"][pl.ds(which + HD, thin), :]
    grad = r["grad"]

    def body(c, _):
        r["arrive"](c)
        out = jnp.dot(r["turned"][...], r["rows"][c], preferred_element_type=F32) * scale
        grad[c % 4, c // 4] = out.astype(BF)
        return 0

    lax.fori_loop(0, 8, body, 0)
    index = lambda ref, i: ref.at[i]
    ring = ring_reduce(
        link, z, up, down, lambda q: grad.at[q], index, r["z_low"], r["z_high"], r["z_full_low"], r["z_full_high"]
    )
    next(ring)
    yield
    next(ring)
    yield
    finish(ring)
    mine = grad.at[z]
    mine[...] = (
        mine[...].astype(F32) + r["z_full_low"][...].astype(F32) + r["z_full_high"][...].astype(F32)
    ).astype(BF)
    s = link.slot()
    link.start(s, mine.at[1 - xl], r["beside"], beside)
    yield
    link.wait(s, r["beside"], beside)
    summed = mine[xl].astype(F32) + r["beside"][...].astype(F32)
    r["summed"][...] = summed
    square = jnp.sum(summed * summed, axis=0, keepdims=True)
    square = jnp.sum(square, axis=1, keepdims=True)
    x = xh * 2 + xl
    stages = (
        [device(core=1 - core)],
        [device(x=lax.rem(x + i, 4)) for i in (1, 2, 3)],
        [device(y=lax.rem(y + i, 4)) for i in (1, 2, 3)],
        [device(z=lax.rem(z + i, 4)) for i in (1, 2, 3)],
    )
    total = jnp.broadcast_to(square, (8, HD))
    for k, others in enumerate(stages):
        r["square"][k] = total
        slots = [link.slot() for _ in others]
        for i, other in enumerate(others):
            link.start(slots[i], r["square"].at[k], r["squares"].at[k, i], other)
        yield
        for i, other in enumerate(others):
            back = others[len(others) - 1 - i]
            link.wait(slots[i], r["squares"].at[k, i], back)
            total = total + r["squares"][k, i]
    count_all = 1.0 * D * HD * (HEADS + 2 * KVH)
    factor = lax.rsqrt(total[:1, :1] / count_all + stat_eps)
    moved = keep_rate * r["moment"][...] + r["summed"][...] * factor
    r["next"][...] = moved
    fresh = r["fresh"]
    fresh[z, xl] = (r["own"][...].astype(F32) - learn_rate * moved).astype(BF)
    s = link.slot()
    link.start(s, fresh.at[z, xl], fresh.at[z, xl], beside)
    n = r["own"].shape[0] // 2
    cut = lambda ref, i: ref.at[pl.ds(i * n, n)]
    first = ring_spread(link, z, up, down, lambda q: fresh.at[q, xl], cut)
    next(first)
    yield
    link.wait(s, fresh.at[z, 1 - xl], beside)
    second = ring_spread(link, z, up, down, lambda q: fresh.at[q, 1 - xl], cut)
    next(second)
    next(first)
    yield
    finish(first)
    next(second)
    yield
    finish(second)


ROW_NAMES = ("gq", "gkv", "w_query", "w_other", "w_head", "tokens", "gain", "rows_hbm", "moment", "own")
OUT_NAMES = ("grad_tokens", "fresh", "next")


def back_kernel(names, *refs):
    r = dict(zip(names, refs))
    p = place()
    link = Link(r["send"], r["recv"])
    copies = []
    step = r["rows"].shape[2]
    for c in range(8):
        copy = pltpu.make_async_copy(
            r["rows_hbm"].at[:, pl.ds(c * step, step)], r["rows"].at[c], r["load"].at[c]
        )
        copy.start()

    def arrive(c):
        pltpu.make_async_copy(
            r["rows_hbm"].at[:, pl.ds(pl.multiple_of(c * step, step), step)], r["rows"].at[c], r["load"].at[c]
        ).wait()

    r["arrive"] = arrive
    x = p["xh"] * 2 + p["xl"]
    others = [device(core=1 - p["core"])]
    for i in (1, 2, 3):
        others.append(device(x=lax.rem(x + i, 4)))
        others.append(device(y=lax.rem(p["y"] + i, 4)))
        others.append(device(z=lax.rem(p["z"] + i, 4)))
    greet(others)
    rows, weights = rows_chain(r, link, p), weight_chain(r, link, p)
    for which in ORDER:
        next(rows if which == "r" else weights, None)
    finish(rows)
    finish(weights)
    link.drain()


ORDER = "rrrr" + "wrwrwrwrwrw"


def back(gq, gkv, w_query, w_other, w_head, tokens, gain, rows, moment, own):
    length, width = rows.shape
    columns, share = own.shape
    block = length // 16
    halves = (block - LOW, LOW)
    v = pltpu.VMEM
    scratch = dict(
        sib_q=v((8, block, 2 * HD), BF),
        sib_kv=v((8, block, 2 * HD), BF),
        pair_kv=v((8, block, 2 * HD), BF),
        kv_all=v((8, 2, block, 2 * HD), BF),
        cat=v((8, block, 6 * HD), BF),
        part=v((2, 4, block, width), BF),
        part_low=v((3, LOW // 2, width), BF),
        part_high=v((3, LOW // 2, width), BF),
        full_low=v((3, LOW, width), BF),
        full_high=v((3, LOW, width), BF),
        cross=v((4, block - LOW, width), BF),
        cross_top=v((LOW, width), BF),
        rows=v((8, length, width // 8), BF),
        load=pltpu.SemaphoreType.DMA((8,)),
        turned=v((columns, length), BF),
        kv_turned=v((2 * HD, length), BF),
        grad=v((4, 2, columns, share), BF),
        z_low=v((columns, share), BF),
        z_high=v((columns, share), BF),
        z_full_low=v((2, columns, share), BF),
        z_full_high=v((2, columns, share), BF),
        beside=v((columns, share), BF),
        summed=v((columns, share), F32),
        square=v((4, 8, HD), F32),
        squares=v((4, 3, 8, HD), F32),
        send=pltpu.SemaphoreType.DMA((48,)),
        recv=pltpu.SemaphoreType.DMA((48,)),
    )
    whole = pl.BlockSpec(memory_space=pltpu.VMEM)
    names = ROW_NAMES + OUT_NAMES + tuple(scratch)
    return pl.pallas_call(
        functools.partial(back_kernel, names),
        in_specs=[pl.BlockSpec(memory_space=pl.ANY) if n == "rows_hbm" else whole for n in ROW_NAMES],
        out_specs=[whole] * 3,
        out_shape=[
            jax.ShapeDtypeStruct((block, width), BF),
            jax.ShapeDtypeStruct((4, 2, columns, share), BF),
            jax.ShapeDtypeStruct((columns, share), F32),
        ],
        scratch_shapes=list(scratch.values()),
        compiler_params=pltpu.CompilerParams(
            collective_id=1, has_side_effects=True, vmem_limit_bytes=62 * 1024 * 1024
        ),
        name="back",
    )(gq, gkv, w_query, w_other, w_head, tokens, gain, rows, moment, own)


def front_kernel(names, *refs):
    r = dict(zip(names, refs))
    p = place()
    link = Link(r["send"], r["recv"])
    core, y, xh = p["core"], p["y"], p["xh"]
    sib, across = device(core=1 - core), device(xh=1 - xh)
    up, down = device(y=lax.rem(y + 1, 4)), device(y=lax.rem(y + 3, 4))
    odd = lax.rem(y, 2)
    pair = device(y=y + 1 - 2 * odd)
    greet([sib, across, up, down])
    rows, kv = r["rows"], r["kv"]
    block, width = rows.shape[3], rows.shape[4]
    thin = HD // INNER
    mine, other = odd * 2 + core, (1 - odd) * 2 + core
    kv_slots = [link.slot() for _ in range(4)]
    kv[mine] = r["kv_own"][...]
    link.start(kv_slots[0], kv.at[mine], kv.at[mine], pair)
    inputs = r["tokens"][...].astype(F32)
    reciprocal = lax.rsqrt(jnp.mean(inputs * inputs, axis=1, keepdims=True) + norm_eps)
    rows[xh, y, core] = (inputs * reciprocal * r["gain"][...]).astype(BF)
    top, rest = pl.ds(0, LOW), pl.ds(LOW, block - LOW)
    cut = lambda n: (lambda ref, i: ref.at[pl.ds(0 if i == 0 else n // 2, n // 2)])

    def cross(slot, q, at):
        link.start(slot, rows.at[xh, q, core, at], rows.at[xh, q, core, at], across)

    def crossed(slot, q, at):
        link.wait(slot, rows.at[1 - xh, q, core, at], across)

    def to_sib(slot, side, q):
        link.start(slot, rows.at[side, q, core], rows.at[side, q, core], sib)

    def spread(side, at, n):
        return ring_spread(link, y, up, down, lambda q: rows.at[side, q, core, at], cut(n))

    top_slot = link.slot()
    rest_slots = [link.slot() for _ in range(4)]
    sib_slots = [[link.slot() for _ in range(4)] for _ in range(2)]
    q0, q1, q2, q3 = y, lax.rem(y + 1, 4), lax.rem(y + 2, 4), lax.rem(y + 3, 4)
    cross(top_slot, q0, top)
    b_own = spread(xh, rest, block - LOW)
    next(b_own)
    a_own = spread(xh, top, LOW)
    next(a_own)
    cross(rest_slots[0], q0, rest)
    to_sib(sib_slots[0][0], xh, q0)
    link.start(kv_slots[1], kv.at[mine], kv.at[mine], sib)
    link.start(kv_slots[3], r["w_query"], r["w_other"], sib)
    stored = []

    def project(side, q, k):
        which = (0, 1, 2, 3)[k % 4]
        link.wait(sib_slots[k // 4][which], rows.at[side, q, 1 - core], sib)
        copy = pltpu.make_async_copy(rows.at[side, q], r["rows_out"].at[side, q], r["store"].at[k])
        copy.start()
        stored.append(copy)
        acc = r["acc"]
        acc[...] = jnp.zeros_like(acc)
        step = 512

        def body(c, _):
            at = pl.ds(pl.multiple_of(c * step, step), step)
            part = rows[side, q, :, :, at].reshape(2 * block, step)
            acc[:, : 2 * HD] += jnp.dot(part, r["w_query"][at, :], preferred_element_type=F32)
            acc[:, 2 * HD :] += dotg(part, r["kv_out"][:, at], NT)
            return 0

        lax.fori_loop(0, width // step, body, 0)
        scale = width ** (-0.5)
        here = pl.ds(pl.multiple_of((side * 4 + q) * 2 * block, 2 * block), 2 * block)
        cos, sin = r["cos"][here, :], r["sin"][here, :]
        for h in range(2):
            r["query"][here, h * HD : (h + 1) * HD] = rope(
                acc[:, h * HD : (h + 1) * HD] * scale, cos, sin, 1.0
            ).astype(BF)
        r["key"][here, :] = rope(acc[:, 2 * HD : 3 * HD] * scale, cos, sin, 1.0).astype(BF)
        r["value"][here, :] = (acc[:, 3 * HD :] * scale).astype(BF)

    crossed(top_slot, q0, top)
    a_far = spread(1 - xh, top, LOW)
    next(a_far)
    next(b_own)
    cross(rest_slots[1], q1, rest)
    cross(rest_slots[3], q3, rest)
    next(a_own)
    to_sib(sib_slots[0][1], xh, q1)
    to_sib(sib_slots[0][3], xh, q3)
    link.wait(kv_slots[0], kv.at[other], pair)
    link.start(kv_slots[2], kv.at[other], kv.at[other], sib)
    crossed(rest_slots[0], q0, rest)
    to_sib(sib_slots[1][0], 1 - xh, q0)
    finish(b_own)
    cross(rest_slots[2], q2, rest)
    finish(a_own)
    to_sib(sib_slots[0][2], xh, q2)
    next(a_far)
    link.wait(kv_slots[1], kv.at[odd * 2 + 1 - core], sib)
    link.wait(kv_slots[2], kv.at[(1 - odd) * 2 + 1 - core], sib)
    for j in range(INNER):
        r["kv_out"][j * thin : (j + 1) * thin, :] = kv[j, :thin, :]
        r["kv_out"][HD + j * thin : HD + (j + 1) * thin, :] = kv[j, thin:, :]
    project(xh, q0, 0)
    project(xh, q1, 1)
    project(xh, q3, 3)
    project(1 - xh, q0, 4)
    project(xh, q2, 2)
    finish(a_far)
    crossed(rest_slots[1], q1, rest)
    to_sib(sib_slots[1][1], 1 - xh, q1)
    crossed(rest_slots[3], q3, rest)
    to_sib(sib_slots[1][3], 1 - xh, q3)
    crossed(rest_slots[2], q2, rest)
    to_sib(sib_slots[1][2], 1 - xh, q2)
    project(1 - xh, q1, 5)
    project(1 - xh, q3, 7)
    project(1 - xh, q2, 6)
    link.wait(kv_slots[3], r["w_other"], sib)
    for copy in stored:
        copy.wait()
    link.drain()


FRONT_IN = ("tokens", "gain", "w_query", "kv_own", "cos", "sin")
FRONT_OUT = ("query", "key", "value", "rows_out", "w_other", "kv_out")


def front(tokens, gain, w_query, kv_own, cos, sin):
    block, width = tokens.shape
    length = cos.shape[0]
    v = pltpu.VMEM
    shape = jax.ShapeDtypeStruct
    scratch = dict(
        rows=v((2, 4, 2, block, width), BF),
        kv=v((INNER, 2 * HD // INNER, width), BF),
        acc=v((2 * block, 4 * HD), F32),
        store=pltpu.SemaphoreType.DMA((8,)),
        send=pltpu.SemaphoreType.DMA((32,)),
        recv=pltpu.SemaphoreType.DMA((32,)),
    )
    whole = pl.BlockSpec(memory_space=pltpu.VMEM)
    far = pl.BlockSpec(memory_space=pl.ANY)
    return pl.pallas_call(
        functools.partial(front_kernel, FRONT_IN + FRONT_OUT + tuple(scratch)),
        in_specs=[whole] * len(FRONT_IN),
        out_specs=[whole, whole, whole, far, far, whole],
        out_shape=[
            shape((length, 2 * HD), BF),
            shape((length, HD), BF),
            shape((length, HD), BF),
            shape((2, 4, 2, block, width), BF),
            shape(w_query.shape, BF),
            shape((2 * HD, width), BF),
        ],
        scratch_shapes=list(scratch.values()),
        compiler_params=pltpu.CompilerParams(
            collective_id=2, has_side_effects=True, vmem_limit_bytes=60 * 1024 * 1024
        ),
        name="front",
    )(tokens, gain, w_query, kv_own, cos, sin)


def tables(length):
    within = np.arange(HD) // 2
    rates = np.power(np.float32(rope_base), within.astype(np.float32) * np.float32(-2.0 / HD))
    angle = np.arange(length, dtype=np.float32)[:, None] * rates.astype(np.float32)[None, :]
    angle = angle.astype(np.float64)
    return np.cos(angle).astype(np.float32), np.sin(angle).astype(np.float32)


def per_device(
    tokens, cotangent, gain, w_query, w_key, w_value, moment_query, moment_key, moment_value
):
    query_width = w_query.shape[1]
    key_width = w_key.shape[1]
    width = tokens.shape[2]
    cos, sin = tables(cotangent.shape[1])
    kv_own = jnp.concatenate([w_key, w_value], axis=1).T
    query, key, value, rows, w_other, w_head = front(
        tokens[0], gain[None], w_query, kv_own, cos, sin
    )
    length = query.shape[0]
    rows = rows.reshape(length, width)
    attended, grad_query, grad_kv = attention(query, key, value, cotangent[0], cos, sin)
    dp_rank = lax.axis_index(DP)
    share = moment_query.shape[0]
    w_mine = jnp.concatenate([w_query, w_key, w_value], axis=1)
    own = lax.dynamic_slice_in_dim(w_mine, dp_rank * share, share, 0).T
    moment = jnp.concatenate([moment_query, moment_key, moment_value], axis=1).T
    by_block = (8, 2, length // 16, 2 * HD)
    grad_tokens, fresh, moved = back(
        grad_query.reshape(by_block),
        grad_kv.reshape(by_block),
        w_query,
        w_other,
        w_head,
        tokens[0],
        gain[None],
        rows,
        moment,
        own,
    )
    moved = moved.T
    fresh = fresh.transpose(1, 0, 3, 2).reshape(width, -1)
    ends = [query_width, query_width + key_width]
    fresh_query, fresh_key, fresh_value = jnp.split(fresh, ends, axis=1)
    next_query, next_key, next_value = jnp.split(moved, ends, axis=1)
    return (
        attended[None],
        grad_tokens[None],
        fresh_query,
        fresh_key,
        fresh_value,
        next_query,
        next_key,
        next_value,
    )


def solution(mesh):
    torus = Mesh(mesh.devices.reshape(2, 4, 2, 2, 2, 2), ALL)
    placed = (
        P(DP, TENSOR, None),
        P(DP, None, TENSOR),
        P(),
        P(None, TENSOR),
        P(None, TENSOR),
        P(None, TENSOR),
        P(DP, TENSOR),
        P(DP, TENSOR),
        P(DP, TENSOR),
    )
    return jax.shard_map(
        per_device,
        mesh=torus,
        in_specs=placed,
        out_specs=(
            P(DP, None, TENSOR),
            P(DP, TENSOR, None),
            P(None, TENSOR),
            P(None, TENSOR),
            P(None, TENSOR),
            P(DP, TENSOR),
            P(DP, TENSOR),
            P(DP, TENSOR),
        ),
        check_vma=False,
    )
```

```python
import functools
from types import SimpleNamespace

import jax
import jax.numpy as jnp
import numpy as np
from jax import lax
from jax.experimental import pallas as pl
from jax.experimental.pallas import tpu as pltpu
from jax.sharding import Mesh
from jax.sharding import PartitionSpec as P

D = 4096
HEADS = 32
KVH = 4
HD = 128
F32 = jnp.float32
BF = jnp.bfloat16
CHIPS = ("x", "yh", "yl")
TENSOR = ("x", "yh", "yl", "core")
SHARE = ("yl", "core")
DP = ("dp_0", "dp_1")
ALL = ("dp_0", "dp_1", "x", "yh", "yl", "core")

rope_base = 1000000.0
norm_eps = 1e-06
stat_eps = 1e-06
learn_rate = 0.05
keep_rate = 0.9


def rope(x, cos, sin, sign):
    lane = lax.broadcasted_iota(jnp.int32, x.shape, 1)
    nxt = pltpu.roll(x, x.shape[1]-1, 1)
    prv = pltpu.roll(x, 1, 1)
    partner = jnp.where(lane % 2 == 0, -nxt, prv)
    return x*cos + partner*(sin*sign)

NT=(((1,),(1,)),((),()))
TN=(((0,),(0,)),((),()))
def dotg(a,b,dims):
    return lax.dot_general(a,b,dims,preferred_element_type=F32)

def attn_kernel(BQ, TC, hs, q_ref, k_ref, v_ref, do_ref, cos_ref, sin_ref,
                out_ref, gq_ref, gkv_ref, va, s_scr, r_scr, p_scr, dk, dv, m_scr, o_scr, g_scr):
    i = pl.program_id(0)
    n = pl.num_programs(0)
    T = k_ref.shape[0]
    R = 2*BQ
    @pl.when(i == 0)
    def _():
        va[:, :HD] = v_ref[...]
        va[:, HD:] = jnp.ones((T, HD), BF)
        dk[...] = jnp.zeros_like(dk)
        dv[...] = jnp.zeros_like(dv)
    q = jnp.concatenate([q_ref[:, :HD], q_ref[:, HD:]], axis=0)
    do = jnp.concatenate([do_ref[:, :HD], do_ref[:, HD:]], axis=0)
    first = i*BQ
    full = first // TC
    used = (first + BQ + TC - 1)//TC
    m_scr[...] = jnp.full((R, HD), -3e38, F32)
    def lane_max(s):
        m = m_scr[...]
        for j in range(TC//HD):
            m = jnp.maximum(m, s[:, j*HD:(j+1)*HD])
        m_scr[...] = m
    def scores(c):
        ks = k_ref[pl.ds(pl.multiple_of(c*TC, TC), TC), :]
        vs = v_ref[pl.ds(pl.multiple_of(c*TC, TC), TC), :]
        r_scr[c] = dotg(do, vs, NT)
        return dotg(q, ks, NT)
    def body1(c, _):
        s = scores(c)
        s_scr[c] = s
        lane_max(s)
        return 0
    lax.fori_loop(0, full, body1, 0)
    def body1d(c, _):
        s = scores(c)
        row = first + lax.broadcasted_iota(jnp.int32, (R, TC), 0) % BQ
        col = c*TC + lax.broadcasted_iota(jnp.int32, (R, TC), 1)
        s = jnp.where(row >= col, s, -1e30)
        s_scr[c] = s
        lane_max(s)
        return 0
    lax.fori_loop(full, used, body1d, 0)
    c2 = hs * 1.4426950408889634
    m = jnp.max(m_scr[...], axis=1, keepdims=True)
    mb = jnp.broadcast_to(m * c2, (R, HD))
    o_scr[...] = jnp.zeros_like(o_scr)
    def body2(c, _):
        s = s_scr[c]
        p = jnp.concatenate([jnp.exp2(s[:, j*HD:(j+1)*HD]*c2 - mb) for j in range(TC//HD)], axis=1).astype(BF)
        p_scr[c] = p
        o_scr[...] += jnp.dot(p, va[pl.ds(pl.multiple_of(c*TC, TC), TC), :], preferred_element_type=F32)
        return 0
    lax.fori_loop(0, used, body2, 0)
    inv = 1.0 / o_scr[:, HD:]
    o = o_scr[:, :HD] * inv
    out_ref[:, :HD] = o[:BQ].astype(BF)
    out_ref[:, HD:] = o[BQ:].astype(BF)
    dof = do.astype(F32)
    delta = jnp.broadcast_to(jnp.sum(dof*o, axis=1, keepdims=True), (R, HD))
    qn = (q.astype(F32) * (inv*hs)).astype(BF)
    don = (dof*inv).astype(BF)
    g_scr[...] = jnp.zeros_like(g_scr)
    def body3(c, _):
        at = pl.ds(pl.multiple_of(c*TC, TC), TC)
        p = p_scr[c]
        r = r_scr[c]
        pf = p.astype(F32)
        g = jnp.concatenate([pf[:, j*HD:(j+1)*HD]*(r[:, j*HD:(j+1)*HD] - delta) for j in range(TC//HD)], axis=1).astype(BF)
        g_scr[...] += jnp.dot(g, k_ref[at, :], preferred_element_type=F32)
        dk[at, :] += dotg(g, qn, TN)
        dv[at, :] += dotg(p, don, TN)
        return 0
    lax.fori_loop(0, used, body3, 0)
    gq = g_scr[...] * (inv*hs)
    here = pl.ds(pl.multiple_of(first, BQ), BQ)
    cos = cos_ref[here, :]
    sin = sin_ref[here, :]
    gq_ref[:, :HD] = rope(gq[:BQ], cos, sin, -1.0).astype(BF)
    gq_ref[:, HD:] = rope(gq[BQ:], cos, sin, -1.0).astype(BF)
    @pl.when(i == n-1)
    def _():
        gkv_ref[:, :HD] = rope(dk[...], cos_ref[...], sin_ref[...], -1.0).astype(BF)
        gkv_ref[:, HD:] = dv[...].astype(BF)

def attention(q, k, v, do, cos, sin, BQ=512, TC=512):
    T = q.shape[0]
    R = 2*BQ
    whole = pl.BlockSpec((T, HD), lambda i: (0, 0))
    rows = pl.BlockSpec((BQ, 2*HD), lambda i: (i, 0))
    return pl.pallas_call(
        functools.partial(attn_kernel, BQ, TC, HD**-0.5),
        grid=(T//BQ,),
        in_specs=[rows, whole, whole, rows, whole, whole],
        out_specs=[rows, rows, pl.BlockSpec((T, 2*HD), lambda i: (0, 0))],
        out_shape=[jax.ShapeDtypeStruct((T, 2*HD), BF)]*3,
        scratch_shapes=[pltpu.VMEM((T, 2*HD), BF), pltpu.VMEM((T//TC, R, TC), F32), pltpu.VMEM((T//TC, R, TC), F32),
            pltpu.VMEM((T//TC, R, TC), BF), pltpu.VMEM((T, HD), F32), pltpu.VMEM((T, HD), F32),
            pltpu.VMEM((R, HD), F32), pltpu.VMEM((R, 2*HD), F32), pltpu.VMEM((R, HD), F32)],
        compiler_params=pltpu.CompilerParams(vmem_limit_bytes=56*1024*1024),
        name="attention",
    )(q, k, v, do, cos, sin)


MESH_ID = pl.DeviceIdType.MESH
INNER = 4


def place():
    at = lax.axis_index
    return SimpleNamespace(
        xl=at("dp_0"), z=at("dp_1"), xh=at("x"), y=at("yh") * 2 + at("yl"), core=at("core")
    )


def device(**moved):
    names = {}
    for key, value in moved.items():
        if key == "y":
            names["yh"] = value // 2
            names["yl"] = value % 2
        elif key == "x":
            names["x"] = value // 2
            names["dp_0"] = value % 2
        else:
            names[{"xl": "dp_0", "z": "dp_1", "xh": "x", "core": "core"}[key]] = value
    return names


class Link:
    def __init__(self, send, recv):
        self.send, self.recv, self.used, self.sent = send, recv, 0, []

    def slot(self):
        self.used += 1
        return self.used - 1

    def start(self, slot, src, dst, to):
        copy = pltpu.make_async_remote_copy(
            src_ref=src,
            dst_ref=dst,
            send_sem=self.send.at[slot],
            recv_sem=self.recv.at[slot],
            device_id=to,
            device_id_type=MESH_ID,
        )
        copy.start()
        self.sent.append(copy)

    def wait(self, slot, landed, to):
        pltpu.make_async_remote_copy(
            src_ref=landed,
            dst_ref=landed,
            send_sem=self.send.at[slot],
            recv_sem=self.recv.at[slot],
            device_id=to,
            device_id_type=MESH_ID,
        ).wait_recv()

    def drain(self):
        for copy in self.sent:
            copy.wait_send()


def added(ref, other):
    ref[...] = (ref[...].astype(F32) + other[...].astype(F32)).astype(BF)


def ring_reduce(link, me, up, down, piece, half, part_low, part_high, full_low, full_high):
    s = [link.slot() for _ in range(4)]
    far = piece(lax.rem(me + 2, 4))
    link.start(s[0], half(far, 0), part_low, up)
    link.start(s[1], half(far, 1), part_high, down)
    yield
    above = piece(lax.rem(me + 1, 4))
    link.wait(s[0], part_low, down)
    added(half(above, 0), part_low)
    link.start(s[2], above, full_low, up)
    below = piece(lax.rem(me + 3, 4))
    link.wait(s[1], part_high, up)
    added(half(below, 1), part_high)
    link.start(s[3], below, full_high, down)
    yield
    link.wait(s[2], full_low, down)
    link.wait(s[3], full_high, up)


def ring_spread(link, me, up, down, piece, half):
    s = [link.slot() for _ in range(4)]
    mine = piece(me)
    link.start(s[0], mine, mine, up)
    link.start(s[1], mine, mine, down)
    yield
    low, high = piece(lax.rem(me + 3, 4)), piece(lax.rem(me + 1, 4))
    link.wait(s[0], low, down)
    link.start(s[2], half(low, 0), half(low, 0), up)
    link.wait(s[1], high, up)
    link.start(s[3], half(high, 1), half(high, 1), down)
    yield
    far = piece(lax.rem(me + 2, 4))
    link.wait(s[2], half(far, 0), down)
    link.wait(s[3], half(far, 1), up)


def finish(steps):
    for _ in steps:
        pass


def greet(others):
    barrier = pltpu.get_barrier_semaphore()
    for other in others:
        pl.semaphore_signal(barrier, inc=1, device_id=other, device_id_type=MESH_ID)
    pl.semaphore_wait(barrier, len(others))


def cut_at(n, lower):
    return n // 32 * 16 if lower else n - n // 32 * 16


def cut(n, lower):
    at = cut_at(n, lower)
    return lambda ref, i: ref.at[pl.ds(0, at) if i == 0 else pl.ds(at, n - at)]


LOW_FRONT = 64
LOW_BACK = 80


def rows_chain(r, link, p):
    core, y, xh = p.core, p.y, p.xh
    sib, across = device(core=1 - core), device(xh=1 - xh)
    up, down = device(y=lax.rem(y + 1, 4)), device(y=lax.rem(y + 3, 4))
    near = y + 1 - 2 * lax.rem(y, 2)
    pair = device(y=near)
    gq, gkv, sib_q, sib_kv, cat = r.gq, r.gkv, r.sib_q, r.sib_kv, r.cat
    one, two = link.slot(), link.slot()
    link.start(one, gkv.at[:, 1 - core], sib_kv, sib)
    link.start(two, gq.at[:, 1 - core], sib_q, sib)
    yield
    link.wait(one, sib_kv, sib)
    added(sib_kv, gkv.at[:, core])
    three = link.slot()
    odd = lax.rem(y, 2)
    half = HD // 2

    def columns(first):
        picks = [sib_kv[:, :, at + first : at + first + half] for at in (0, HD)]
        return jnp.concatenate(picks, axis=2)

    low, high_half = columns(0), columns(half)
    r.kv_out[...] = jnp.where(odd == 1, low, high_half)
    r.kv_keep[...] = jnp.where(odd == 1, high_half, low)
    link.start(three, r.kv_out, r.pair_kv, pair)
    link.wait(two, sib_q, sib)
    cat[:, :, : 2 * HD] = gq[:, core]
    cat[:, :, 2 * HD : 4 * HD] = sib_q[...]
    cat[:, :, 4 * HD :] = sib_kv[...]
    rows = 4 * cat.shape[1]
    width = r.part.shape[3]
    step = 512
    scale = width ** (-0.5)

    def products(side):
        left = cat[pl.ds(side * 4, 4)].reshape(rows, 6 * HD)

        def body(c, _):
            at = pl.ds(pl.multiple_of(c * step, step), step)
            out = dotg(left[:, : 2 * HD], r.w_query[at, :], NT)
            out = out + dotg(left[:, 2 * HD : 4 * HD], r.w_other[at, :], NT)
            out = out + jnp.dot(left[:, 4 * HD :], r.w_head[:, at], preferred_element_type=F32)
            out = out * scale
            r.part[side, :, :, at] = out.astype(BF).reshape(4, rows // 4, step)
            return 0

        lax.fori_loop(0, width // step, body, 0)

    part = r.part
    high = part.shape[2] - LOW_BACK
    top, rest = pl.ds(0, LOW_BACK), pl.ds(LOW_BACK, high)

    def ring(side, rows_at, n, bufs):
        return ring_reduce(
            link, y, up, down, lambda q: part.at[side, q, rows_at], cut(n, rows_at is rest), *bufs
        )

    def bufs(k):
        n = (LOW_BACK, LOW_BACK, high)[k]
        first = cut_at(n, k == 2)
        sizes = (first, n - first, n, n)
        refs = (r.part_low, r.part_high, r.full_low, r.full_high)
        return tuple(ref.at[k, pl.ds(0, size)] for ref, size in zip(refs, sizes))

    products(1 - xh)
    across_slots = [link.slot() for _ in range(4)]
    order = [lax.rem(y + i, 4) for i in (2, 1, 3, 0)]
    for i, q in enumerate(order):
        link.start(across_slots[i], part.at[1 - xh, q, rest], r.cross.at[q], across)
    far_ring = ring(1 - xh, top, LOW_BACK, bufs(0))
    next(far_ring)
    products(xh)
    near_ring = ring(xh, top, LOW_BACK, bufs(1))
    next(near_ring)
    yield
    link.wait(three, r.pair_kv, pair)
    total = (r.kv_keep[...].astype(F32) + r.pair_kv[...].astype(F32)).astype(BF)
    r.kv_all[:, core] = total
    four = link.slot()
    link.start(four, r.kv_all.at[:, core], r.kv_all.at[:, core], sib)
    next(far_ring)
    link.wait(four, r.kv_all.at[:, 1 - core], sib)
    yield
    next(near_ring)
    yield
    finish(far_ring)
    k = 0
    done = part.at[1 - xh, y, top]
    done[...] = (
        done[...].astype(F32)
        + r.full_low[k, :LOW_BACK].astype(F32)
        + r.full_high[k, :LOW_BACK].astype(F32)
    ).astype(BF)
    last = link.slot()
    link.start(last, done, r.cross_top, across)
    yield
    def crossed(i):
        link.wait(across_slots[i], r.cross.at[order[i]], across)
        added(part.at[xh, order[i], rest], r.cross.at[order[i]])

    crossed(0)
    rest_ring = ring(xh, rest, high, bufs(2))
    next(rest_ring)
    yield
    crossed(1)
    crossed(2)
    finish(near_ring)
    next(rest_ring)
    yield
    crossed(3)
    finish(rest_ring)
    link.wait(last, r.cross_top, across)
    own = part.at[xh, y]
    top_rows = (
        own[top].astype(F32)
        + r.full_low[1, :LOW_BACK].astype(F32)
        + r.full_high[1, :LOW_BACK].astype(F32)
        + r.cross_top[...].astype(F32)
    )
    rest_rows = (
        own[rest].astype(F32)
        + r.full_low[2, :high].astype(F32)
        + r.full_high[2, :high].astype(F32)
    )
    for first, grad_normed in ((0, top_rows), (LOW_BACK, rest_rows)):
        at = pl.ds(first, grad_normed.shape[0])
        inputs = r.tokens[at, :].astype(F32)
        reciprocal = lax.rsqrt(jnp.mean(inputs * inputs, axis=1, keepdims=True) + norm_eps)
        unit = inputs * reciprocal
        grad_unit = grad_normed * r.gain[...]
        inner = jnp.mean(grad_unit * unit, axis=1, keepdims=True)
        r.grad_tokens[at, :] = (reciprocal * (grad_unit - unit * inner)).astype(BF)


def weight_chain(r, link, p):
    core, y, xh, xl, z = p.core, p.y, p.xh, p.xl, p.z
    up, down = device(z=lax.rem(z + 1, 4)), device(z=lax.rem(z + 3, 4))
    beside = device(xl=1 - xl)
    wide = 2 * HD
    thin = HD // INNER
    length = r.turned.shape[1]
    share = r.rows.shape[2]
    width = 8 * share
    scale = width ** (-0.5)
    index = lambda ref, i: ref.at[i]
    chains = ("q", "kv")

    def ring(n):
        grad = getattr(r, n + "_grad")
        bufs = [getattr(r, n + end) for end in ("_low", "_high", "_full_low", "_full_high")]
        return ring_reduce(link, z, up, down, lambda q: grad.at[q], index, *bufs)

    r.turned[...] = r.gq[...].reshape(length, wide).T

    def query_part(c, _):
        r.arrive(c)
        out = jnp.dot(r.turned[...], r.rows[c], preferred_element_type=F32) * scale
        r.q_grad[lax.rem(c, 4), c // 4] = out.T.astype(BF)
        return 0

    lax.fori_loop(0, 8, query_part, 0)
    rings = {"q": ring("q")}
    next(rings["q"])
    yield
    which = pl.multiple_of(core * thin, thin)
    r.turned[:HD, :] = r.kv_all[...].reshape(length, HD).T
    r.kv_turned[:thin, :] = r.turned[pl.ds(which, thin), :]
    r.kv_turned[thin:, :] = r.turned[pl.ds(which + HD // 2, thin), :]

    def kv_part(c, _):
        out = jnp.dot(r.kv_turned[...], r.rows[c], preferred_element_type=F32) * scale
        r.kv_grad[lax.rem(c, 4), c // 4] = out.astype(BF)
        return 0

    lax.fori_loop(0, 8, kv_part, 0)
    rings["kv"] = ring("kv")
    next(rings["kv"])
    yield
    next(rings["q"])
    yield
    next(rings["kv"])
    yield
    slots = {}
    for n in chains:
        finish(rings[n])
        mine = getattr(r, n + "_grad").at[z]
        for i in range(2):
            mine[i] = (
                mine[i].astype(F32)
                + getattr(r, n + "_full_low")[i].astype(F32)
                + getattr(r, n + "_full_high")[i].astype(F32)
            ).astype(BF)
        slots[n] = link.slot()
        link.start(slots[n], mine.at[1 - xl], getattr(r, n + "_beside"), beside)
    yield
    square = jnp.zeros((1, 1), F32)
    for n in chains:
        link.wait(slots[n], getattr(r, n + "_beside"), beside)
        summed = getattr(r, n + "_grad")[z, xl].astype(F32) + getattr(r, n + "_beside")[...].astype(F32)
        getattr(r, n + "_summed")[...] = summed
        part = jnp.sum(summed * summed, axis=0, keepdims=True)
        square = square + jnp.sum(part, axis=1, keepdims=True)
    x = xh * 2 + xl
    stages = (
        [device(core=1 - core)],
        [device(x=lax.rem(x + i, 4)) for i in (1, 2, 3)],
        [device(y=lax.rem(y + i, 4)) for i in (1, 2, 3)],
        [device(z=lax.rem(z + i, 4)) for i in (1, 2, 3)],
    )
    total = jnp.broadcast_to(square, (8, HD))
    for k, others in enumerate(stages):
        r.square[k] = total
        slot = [link.slot() for _ in others]
        for i, other in enumerate(others):
            link.start(slot[i], r.square.at[k], r.squares.at[k, i], other)
        yield
        for i, other in enumerate(others):
            link.wait(slot[i], r.squares.at[k, i], other)
            total = total + r.squares[k, i]
    count_all = 1.0 * D * HD * (HEADS + 2 * KVH)
    factor = lax.rsqrt(total[:1, :1] / count_all + stat_eps)

    def place_of(q, side):
        return pl.ds(pl.multiple_of((side * 4 + q) * share, share), share)

    here = place_of(z, xl)
    moved = keep_rate * r.moment_q[...] + r.q_summed[...] * factor
    r.next_q[...] = moved
    r.fresh_q[here, :] = (r.w_query[here, :].astype(F32) - learn_rate * moved).astype(BF)
    views = {"q": lambda q, side: r.fresh_q.at[place_of(q, side)]}
    cuts = {"q": lambda ref, i: ref.at[pl.ds(i * share // 2, share // 2)]}
    moved = keep_rate * r.moment_kv[...] + r.kv_summed[...] * factor
    r.next_kv[...] = moved
    r.fresh_kv[:, here] = (r.kv_own[:, here].astype(F32) - learn_rate * moved).astype(BF)
    views["kv"] = lambda q, side: r.fresh_kv.at[:, place_of(q, side)]
    cuts["kv"] = lambda ref, i: ref.at[pl.ds(i * thin, thin)]

    def spread(n, side):
        return ring_spread(link, z, up, down, lambda q: views[n](q, side), cuts[n])

    first, second = [], []
    for n in chains:
        slots[n] = link.slot()
        link.start(slots[n], views[n](z, xl), views[n](z, xl), beside)
        first.append(spread(n, xl))
        next(first[-1])
    yield
    for n in chains:
        link.wait(slots[n], views[n](z, 1 - xl), beside)
        second.append(spread(n, 1 - xl))
        next(second[-1])
    yield
    for s in first:
        next(s)
    yield
    for s in second:
        next(s)
    yield
    for s in first + second:
        finish(s)


def back_kernel(names, *refs):
    r = SimpleNamespace(**dict(zip(names, refs)))
    p = place()
    link = Link(r.send, r.recv)
    step = r.rows.shape[2]
    for c in range(8):
        pltpu.make_async_copy(
            r.rows_hbm.at[:, pl.ds(c * step, step)], r.rows.at[c], r.load.at[c]
        ).start()

    def arrive(c):
        pltpu.make_async_copy(
            r.rows_hbm.at[:, pl.ds(pl.multiple_of(c * step, step), step)], r.rows.at[c], r.load.at[c]
        ).wait()

    r.arrive = arrive
    x = p.xh * 2 + p.xl
    others = [device(core=1 - p.core)]
    for i in (1, 2, 3):
        others.append(device(x=lax.rem(x + i, 4)))
        others.append(device(y=lax.rem(p.y + i, 4)))
        others.append(device(z=lax.rem(p.z + i, 4)))
    greet(others)
    rows, weights = rows_chain(r, link, p), weight_chain(r, link, p)
    for which in ORDER:
        next(rows if which == "r" else weights, None)
    finish(rows)
    finish(weights)
    link.drain()


ORDER = "rwrrwwwrwrwwrwwrwwrww"


def back(gq, gkv, w_query, w_other, w_head, kv_own, tokens, gain, rows, moment_q, moment_kv):
    length, width = rows.shape
    share, wide = moment_q.shape
    few = moment_kv.shape[0]
    block = length // 16
    most = max(LOW_BACK, block - LOW_BACK)
    v = pltpu.VMEM
    shape = jax.ShapeDtypeStruct
    ins = dict(
        gq=gq,
        gkv=gkv,
        w_query=w_query,
        w_other=w_other,
        w_head=w_head,
        kv_own=kv_own,
        tokens=tokens,
        gain=gain,
        rows_hbm=rows,
        moment_q=moment_q,
        moment_kv=moment_kv,
    )
    outs = dict(
        grad_tokens=shape((block, width), BF),
        fresh_q=shape(w_query.shape, BF),
        fresh_kv=shape((few, width), BF),
        next_q=shape(moment_q.shape, F32),
        next_kv=shape(moment_kv.shape, F32),
    )
    scratch = dict(
        sib_q=v((8, block, wide), BF),
        sib_kv=v((8, block, wide), BF),
        pair_kv=v((8, block, HD), BF),
        kv_out=v((8, block, HD), BF),
        kv_keep=v((8, block, HD), BF),
        kv_all=v((8, 2, block, HD), BF),
        cat=v((8, block, 3 * wide), BF),
        part=v((2, 4, block, width), BF),
        part_low=v((3, most // 32 * 16 + 16, width), BF),
        part_high=v((3, most // 32 * 16 + 16, width), BF),
        full_low=v((3, most, width), BF),
        full_high=v((3, most, width), BF),
        cross=v((4, block - LOW_BACK, width), BF),
        cross_top=v((LOW_BACK, width), BF),
        rows=v((8, length, share), BF),
        load=pltpu.SemaphoreType.DMA((8,)),
        turned=v((wide, length), BF),
        kv_turned=v((few, length), BF),
        square=v((4, 8, HD), F32),
        squares=v((4, 3, 8, HD), F32),
        send=pltpu.SemaphoreType.DMA((64,)),
        recv=pltpu.SemaphoreType.DMA((64,)),
    )
    for n, dims in (("q", (share, wide)), ("kv", (few, share))):
        scratch[n + "_grad"] = v((4, 2, *dims), BF)
        scratch[n + "_low"] = v(dims, BF)
        scratch[n + "_high"] = v(dims, BF)
        scratch[n + "_full_low"] = v((2, *dims), BF)
        scratch[n + "_full_high"] = v((2, *dims), BF)
        scratch[n + "_beside"] = v(dims, BF)
        scratch[n + "_summed"] = v(dims, F32)
    whole = pl.BlockSpec(memory_space=pltpu.VMEM)
    far = pl.BlockSpec(memory_space=pl.ANY)
    return pl.pallas_call(
        functools.partial(back_kernel, tuple(ins) + tuple(outs) + tuple(scratch)),
        in_specs=[far if n == "rows_hbm" else whole for n in ins],
        out_specs=[whole] * len(outs),
        out_shape=list(outs.values()),
        scratch_shapes=list(scratch.values()),
        compiler_params=pltpu.CompilerParams(
            collective_id=1, has_side_effects=True, vmem_limit_bytes=62 * 1024 * 1024
        ),
        name="back",
    )(*ins.values())

def front_kernel(names, *refs):
    r = SimpleNamespace(**dict(zip(names, refs)))
    p = place()
    link = Link(r.send, r.recv)
    core, y, xh = p.core, p.y, p.xh
    sib, across = device(core=1 - core), device(xh=1 - xh)
    up, down = device(y=lax.rem(y + 1, 4)), device(y=lax.rem(y + 3, 4))
    odd = lax.rem(y, 2)
    pair = device(y=y + 1 - 2 * odd)
    z = p.z
    z_up, z_down = device(z=lax.rem(z + 1, 4)), device(z=lax.rem(z + 3, 4))
    greet([sib, across, up, down, z_up, z_down])
    rows, kv = r.rows, r.kv
    block, width = rows.shape[3], rows.shape[4]
    thin = HD // INNER
    mine, other = odd * 2 + core, (1 - odd) * 2 + core
    kv_slots = [link.slot() for _ in range(4)]
    quarter = kv.shape[1] // 4

    def kv_piece(which):
        return lambda q: kv.at[which, pl.ds(pl.multiple_of(q * quarter, quarter), quarter)]

    kv[mine] = r.kv_own[...]
    link.start(kv_slots[0], kv_piece(mine)(z), kv_piece(mine)(z), pair)
    inputs = r.tokens[...].astype(F32)
    reciprocal = lax.rsqrt(jnp.mean(inputs * inputs, axis=1, keepdims=True) + norm_eps)
    rows[xh, y, core] = (inputs * reciprocal * r.gain[...]).astype(BF)
    top, rest = pl.ds(0, LOW_FRONT), pl.ds(LOW_FRONT, block - LOW_FRONT)

    def cross(slot, q, at):
        link.start(slot, rows.at[xh, q, core, at], rows.at[xh, q, core, at], across)

    def crossed(slot, q, at):
        link.wait(slot, rows.at[1 - xh, q, core, at], across)

    def to_sib(slot, side, q):
        link.start(slot, rows.at[side, q, core], rows.at[side, q, core], sib)

    def spread(side, at, n):
        return ring_spread(link, y, up, down, lambda q: rows.at[side, q, core, at], cut(n, at is rest))

    top_slot = link.slot()
    rest_slots = [link.slot() for _ in range(4)]
    sib_slots = [[link.slot() for _ in range(4)] for _ in range(2)]
    q0, q1, q2, q3 = y, lax.rem(y + 1, 4), lax.rem(y + 2, 4), lax.rem(y + 3, 4)
    cross(top_slot, q0, top)
    b_own = spread(xh, rest, block - LOW_FRONT)
    next(b_own)
    a_own = spread(xh, top, LOW_FRONT)
    next(a_own)
    cross(rest_slots[0], q0, rest)
    to_sib(sib_slots[0][0], xh, q0)
    link.start(kv_slots[1], kv.at[mine], kv.at[mine], sib)
    link.start(kv_slots[3], r.w_query, r.w_other, sib)
    stored = []

    def project(side, q, k):
        which = (0, 1, 2, 3)[k % 4]
        link.wait(sib_slots[k // 4][which], rows.at[side, q, 1 - core], sib)
        copy = pltpu.make_async_copy(rows.at[side, q], r.rows_out.at[side, q], r.store.at[k])
        copy.start()
        stored.append(copy)
        acc = r.acc
        acc[...] = jnp.zeros_like(acc)
        step = 512

        def body(c, _):
            at = pl.ds(pl.multiple_of(c * step, step), step)
            part = rows[side, q, :, :, at].reshape(2 * block, step)
            acc[:, : 2 * HD] += jnp.dot(part, r.w_query[at, :], preferred_element_type=F32)
            acc[:, 2 * HD :] += dotg(part, r.kv_out[:, at], NT)
            return 0

        lax.fori_loop(0, width // step, body, 0)
        scale = width ** (-0.5)
        here = pl.ds(pl.multiple_of((side * 4 + q) * 2 * block, 2 * block), 2 * block)
        cos, sin = r.cos[here, :], r.sin[here, :]
        for h in range(2):
            r.query[here, h * HD : (h + 1) * HD] = rope(
                acc[:, h * HD : (h + 1) * HD] * scale, cos, sin, 1.0
            ).astype(BF)
        r.key[here, :] = rope(acc[:, 2 * HD : 3 * HD] * scale, cos, sin, 1.0).astype(BF)
        r.value[here, :] = (acc[:, 3 * HD :] * scale).astype(BF)

    link.wait(kv_slots[0], kv_piece(other)(z), pair)
    sides = lambda ref, i: ref.at[:, pl.ds(i * (width // 2), width // 2)]
    kv_ring = ring_spread(link, z, z_up, z_down, kv_piece(other), sides)
    next(kv_ring)
    next(kv_ring)
    finish(kv_ring)
    link.start(kv_slots[2], kv.at[other], kv.at[other], sib)
    crossed(top_slot, q0, top)
    a_far = spread(1 - xh, top, LOW_FRONT)
    next(a_far)
    next(b_own)
    cross(rest_slots[1], q1, rest)
    cross(rest_slots[3], q3, rest)
    next(a_own)
    to_sib(sib_slots[0][1], xh, q1)
    to_sib(sib_slots[0][3], xh, q3)
    crossed(rest_slots[0], q0, rest)
    to_sib(sib_slots[1][0], 1 - xh, q0)
    finish(b_own)
    cross(rest_slots[2], q2, rest)
    finish(a_own)
    to_sib(sib_slots[0][2], xh, q2)
    next(a_far)
    link.wait(kv_slots[1], kv.at[odd * 2 + 1 - core], sib)
    link.wait(kv_slots[2], kv.at[(1 - odd) * 2 + 1 - core], sib)
    for j in range(INNER):
        r.kv_out[j * thin : (j + 1) * thin, :] = kv[j, :thin, :]
        r.kv_out[HD + j * thin : HD + (j + 1) * thin, :] = kv[j, thin:, :]
    project(xh, q0, 0)
    project(xh, q1, 1)
    project(xh, q3, 3)
    project(1 - xh, q0, 4)
    project(xh, q2, 2)
    finish(a_far)
    crossed(rest_slots[1], q1, rest)
    to_sib(sib_slots[1][1], 1 - xh, q1)
    crossed(rest_slots[3], q3, rest)
    to_sib(sib_slots[1][3], 1 - xh, q3)
    crossed(rest_slots[2], q2, rest)
    to_sib(sib_slots[1][2], 1 - xh, q2)
    project(1 - xh, q1, 5)
    project(1 - xh, q3, 7)
    project(1 - xh, q2, 6)
    link.wait(kv_slots[3], r.w_other, sib)
    for copy in stored:
        copy.wait()
    link.drain()


def front(tokens, gain, w_query, kv_own, cos, sin):
    block, width = tokens.shape
    length = cos.shape[0]
    v = pltpu.VMEM
    shape = jax.ShapeDtypeStruct
    ins = dict(tokens=tokens, gain=gain, w_query=w_query, kv_own=kv_own, cos=cos, sin=sin)
    outs = dict(
        query=shape((length, 2 * HD), BF),
        key=shape((length, HD), BF),
        value=shape((length, HD), BF),
        rows_out=shape((2, 4, 2, block, width), BF),
        w_other=shape(w_query.shape, BF),
        kv_out=shape((2 * HD, width), BF),
    )
    scratch = dict(
        rows=v((2, 4, 2, block, width), BF),
        kv=v((INNER, 2 * HD // INNER, width), BF),
        acc=v((2 * block, 4 * HD), F32),
        store=pltpu.SemaphoreType.DMA((8,)),
        send=pltpu.SemaphoreType.DMA((40,)),
        recv=pltpu.SemaphoreType.DMA((40,)),
    )
    whole = pl.BlockSpec(memory_space=pltpu.VMEM)
    far = pl.BlockSpec(memory_space=pl.ANY)
    return pl.pallas_call(
        functools.partial(front_kernel, tuple(ins) + tuple(outs) + tuple(scratch)),
        in_specs=[whole] * len(ins),
        out_specs=[whole, whole, whole, far, far, whole],
        out_shape=list(outs.values()),
        scratch_shapes=list(scratch.values()),
        compiler_params=pltpu.CompilerParams(
            collective_id=2, has_side_effects=True, vmem_limit_bytes=60 * 1024 * 1024
        ),
        name="front",
    )(*ins.values())


def tables(length):
    within = np.arange(HD) // 2
    rates = np.power(np.float32(rope_base), within.astype(np.float32) * np.float32(-2.0 / HD))
    angle = np.arange(length, dtype=np.float32)[:, None] * rates.astype(np.float32)[None, :]
    angle = angle.astype(np.float64)
    return np.cos(angle).astype(np.float32), np.sin(angle).astype(np.float32)


def per_device(
    tokens, cotangent, gain, w_query, w_key, w_value, moment_query, moment_key, moment_value
):
    key_width = w_key.shape[1]
    width = tokens.shape[2]
    cos, sin = tables(cotangent.shape[1])
    kv_own = jnp.concatenate([w_key, w_value], axis=1).T
    query, key, value, rows, w_other, w_head = front(
        tokens[0], gain[None], w_query, kv_own, cos, sin
    )
    length = query.shape[0]
    rows = rows.reshape(length, width)
    attended, grad_query, grad_kv = attention(query, key, value, cotangent[0], cos, sin)
    by_block = (8, 2, length // 16, 2 * HD)
    grad_tokens, fresh_query, fresh_kv, next_query, next_kv = back(
        grad_query.reshape(by_block),
        grad_kv.reshape(by_block),
        w_query,
        w_other,
        w_head,
        kv_own,
        tokens[0],
        gain[None],
        rows,
        moment_query,
        jnp.concatenate([moment_key, moment_value], axis=1).T,
    )
    fresh_key, fresh_value = fresh_kv[:key_width].T, fresh_kv[key_width:].T
    next_key, next_value = next_kv[:key_width].T, next_kv[key_width:].T
    return (
        attended[None],
        grad_tokens[None],
        fresh_query,
        fresh_key,
        fresh_value,
        next_query,
        next_key,
        next_value,
    )


def solution(mesh):
    torus = Mesh(mesh.devices.reshape(2, 4, 2, 2, 2, 2), ALL)
    placed = (
        P(DP, TENSOR, None),
        P(DP, None, TENSOR),
        P(),
        P(None, TENSOR),
        P(None, TENSOR),
        P(None, TENSOR),
        P(DP, TENSOR),
        P(DP, TENSOR),
        P(DP, TENSOR),
    )
    return jax.shard_map(
        per_device,
        mesh=torus,
        in_specs=placed,
        out_specs=(
            P(DP, None, TENSOR),
            P(DP, TENSOR, None),
            P(None, TENSOR),
            P(None, TENSOR),
            P(None, TENSOR),
            P(DP, TENSOR),
            P(DP, TENSOR),
            P(DP, TENSOR),
        ),
        check_vma=False,
    )
```

```python
import functools
from types import SimpleNamespace

import jax
import jax.numpy as jnp
import numpy as np
from jax import lax
from jax.experimental import pallas as pl
from jax.experimental.pallas import tpu as pltpu
from jax.sharding import Mesh
from jax.sharding import PartitionSpec as P

D = 4096
HEADS = 32
KVH = 4
HD = 128
F32 = jnp.float32
BF = jnp.bfloat16
CHIPS = ("x", "yh", "yl")
TENSOR = ("x", "yh", "yl", "core")
SHARE = ("yl", "core")
DP = ("dp_0", "dp_1")
ALL = ("dp_0", "dp_1", "x", "yh", "yl", "core")

rope_base = 1000000.0
norm_eps = 1e-06
stat_eps = 1e-06
learn_rate = 0.05
keep_rate = 0.9


def rope(x, cos, sin, sign):
    lane = lax.broadcasted_iota(jnp.int32, x.shape, 1)
    nxt = pltpu.roll(x, x.shape[1]-1, 1)
    prv = pltpu.roll(x, 1, 1)
    partner = jnp.where(lane % 2 == 0, -nxt, prv)
    return x*cos + partner*(sin*sign)

NT=(((1,),(1,)),((),()))
TN=(((0,),(0,)),((),()))
def dotg(a,b,dims):
    return lax.dot_general(a,b,dims,preferred_element_type=F32)

def attn_kernel(BQ, TC, hs, q_ref, k_ref, v_ref, do_ref, cos_ref, sin_ref,
                out_ref, gq_ref, gkv_ref, va, s_scr, r_scr, p_scr, dk, dv, m_scr, o_scr, g_scr):
    i = pl.program_id(0)
    n = pl.num_programs(0)
    T = k_ref.shape[0]
    R = 2*BQ
    @pl.when(i == 0)
    def _():
        va[:, :HD] = v_ref[...]
        va[:, HD:] = jnp.ones((T, HD), BF)
        dk[...] = jnp.zeros_like(dk)
        dv[...] = jnp.zeros_like(dv)
    q = jnp.concatenate([q_ref[:, :HD], q_ref[:, HD:]], axis=0)
    do = jnp.concatenate([do_ref[:, :HD], do_ref[:, HD:]], axis=0)
    first = i*BQ
    full = first // TC
    used = (first + BQ + TC - 1)//TC
    m_scr[...] = jnp.full((R, HD), -3e38, F32)
    def lane_max(s):
        m = m_scr[...]
        for j in range(TC//HD):
            m = jnp.maximum(m, s[:, j*HD:(j+1)*HD])
        m_scr[...] = m
    def scores(c):
        ks = k_ref[pl.ds(pl.multiple_of(c*TC, TC), TC), :]
        vs = v_ref[pl.ds(pl.multiple_of(c*TC, TC), TC), :]
        r_scr[c] = dotg(do, vs, NT)
        return dotg(q, ks, NT)
    def body1(c, _):
        s = scores(c)
        s_scr[c] = s
        lane_max(s)
        return 0
    lax.fori_loop(0, full, body1, 0)
    def body1d(c, _):
        s = scores(c)
        row = first + lax.broadcasted_iota(jnp.int32, (R, TC), 0) % BQ
        col = c*TC + lax.broadcasted_iota(jnp.int32, (R, TC), 1)
        s = jnp.where(row >= col, s, -1e30)
        s_scr[c] = s
        lane_max(s)
        return 0
    lax.fori_loop(full, used, body1d, 0)
    c2 = hs * 1.4426950408889634
    m = jnp.max(m_scr[...], axis=1, keepdims=True)
    mb = jnp.broadcast_to(m * c2, (R, HD))
    o_scr[...] = jnp.zeros_like(o_scr)
    def body2(c, _):
        s = s_scr[c]
        p = jnp.concatenate([jnp.exp2(s[:, j*HD:(j+1)*HD]*c2 - mb) for j in range(TC//HD)], axis=1).astype(BF)
        p_scr[c] = p
        o_scr[...] += jnp.dot(p, va[pl.ds(pl.multiple_of(c*TC, TC), TC), :], preferred_element_type=F32)
        return 0
    lax.fori_loop(0, used, body2, 0)
    inv = 1.0 / o_scr[:, HD:]
    o = o_scr[:, :HD] * inv
    out_ref[:, :HD] = o[:BQ].astype(BF)
    out_ref[:, HD:] = o[BQ:].astype(BF)
    dof = do.astype(F32)
    delta = jnp.broadcast_to(jnp.sum(dof*o, axis=1, keepdims=True), (R, HD))
    qn = (q.astype(F32) * (inv*hs)).astype(BF)
    don = (dof*inv).astype(BF)
    g_scr[...] = jnp.zeros_like(g_scr)
    def body3(c, _):
        at = pl.ds(pl.multiple_of(c*TC, TC), TC)
        p = p_scr[c]
        r = r_scr[c]
        pf = p.astype(F32)
        g = jnp.concatenate([pf[:, j*HD:(j+1)*HD]*(r[:, j*HD:(j+1)*HD] - delta) for j in range(TC//HD)], axis=1).astype(BF)
        g_scr[...] += jnp.dot(g, k_ref[at, :], preferred_element_type=F32)
        dk[at, :] += dotg(g, qn, TN)
        dv[at, :] += dotg(p, don, TN)
        return 0
    lax.fori_loop(0, used, body3, 0)
    gq = g_scr[...] * (inv*hs)
    here = pl.ds(pl.multiple_of(first, BQ), BQ)
    cos = cos_ref[here, :]
    sin = sin_ref[here, :]
    gq_ref[:, :HD] = rope(gq[:BQ], cos, sin, -1.0).astype(BF)
    gq_ref[:, HD:] = rope(gq[BQ:], cos, sin, -1.0).astype(BF)
    @pl.when(i == n-1)
    def _():
        gkv_ref[:, :HD] = rope(dk[...], cos_ref[...], sin_ref[...], -1.0).astype(BF)
        gkv_ref[:, HD:] = dv[...].astype(BF)

def attention(q, k, v, do, cos, sin, BQ=512, TC=512):
    T = q.shape[0]
    R = 2*BQ
    whole = pl.BlockSpec((T, HD), lambda i: (0, 0))
    rows = pl.BlockSpec((BQ, 2*HD), lambda i: (i, 0))
    return pl.pallas_call(
        functools.partial(attn_kernel, BQ, TC, HD**-0.5),
        grid=(T//BQ,),
        in_specs=[rows, whole, whole, rows, whole, whole],
        out_specs=[rows, rows, pl.BlockSpec((T, 2*HD), lambda i: (0, 0))],
        out_shape=[jax.ShapeDtypeStruct((T, 2*HD), BF)]*3,
        scratch_shapes=[pltpu.VMEM((T, 2*HD), BF), pltpu.VMEM((T//TC, R, TC), F32), pltpu.VMEM((T//TC, R, TC), F32),
            pltpu.VMEM((T//TC, R, TC), BF), pltpu.VMEM((T, HD), F32), pltpu.VMEM((T, HD), F32),
            pltpu.VMEM((R, HD), F32), pltpu.VMEM((R, 2*HD), F32), pltpu.VMEM((R, HD), F32)],
        compiler_params=pltpu.CompilerParams(vmem_limit_bytes=56*1024*1024),
        name="attention",
    )(q, k, v, do, cos, sin)


MESH_ID = pl.DeviceIdType.MESH
INNER = 4


def place():
    at = lax.axis_index
    return SimpleNamespace(
        xl=at("dp_0"), z=at("dp_1"), xh=at("x"), y=at("yh") * 2 + at("yl"), core=at("core")
    )


def device(**moved):
    names = {}
    for key, value in moved.items():
        if key == "y":
            names["yh"] = value // 2
            names["yl"] = value % 2
        elif key == "x":
            names["x"] = value // 2
            names["dp_0"] = value % 2
        else:
            names[{"xl": "dp_0", "z": "dp_1", "xh": "x", "core": "core"}[key]] = value
    return names


class Link:
    def __init__(self, send, recv):
        self.send, self.recv, self.used, self.sent = send, recv, 0, []

    def slot(self):
        self.used += 1
        return self.used - 1

    def start(self, slot, src, dst, to):
        copy = pltpu.make_async_remote_copy(
            src_ref=src,
            dst_ref=dst,
            send_sem=self.send.at[slot],
            recv_sem=self.recv.at[slot],
            device_id=to,
            device_id_type=MESH_ID,
        )
        copy.start()
        self.sent.append(copy)

    def wait(self, slot, landed, to):
        pltpu.make_async_remote_copy(
            src_ref=landed,
            dst_ref=landed,
            send_sem=self.send.at[slot],
            recv_sem=self.recv.at[slot],
            device_id=to,
            device_id_type=MESH_ID,
        ).wait_recv()

    def drain(self):
        for copy in self.sent:
            copy.wait_send()


def added(ref, other):
    ref[...] = (ref[...].astype(F32) + other[...].astype(F32)).astype(BF)


def ring_reduce(link, me, up, down, piece, half, part_low, part_high, full_low, full_high):
    s = [link.slot() for _ in range(4)]
    far = piece(lax.rem(me + 2, 4))
    link.start(s[0], half(far, 0), part_low, up)
    link.start(s[1], half(far, 1), part_high, down)
    yield
    above = piece(lax.rem(me + 1, 4))
    link.wait(s[0], part_low, down)
    added(half(above, 0), part_low)
    link.start(s[2], above, full_low, up)
    below = piece(lax.rem(me + 3, 4))
    link.wait(s[1], part_high, up)
    added(half(below, 1), part_high)
    link.start(s[3], below, full_high, down)
    yield
    link.wait(s[2], full_low, down)
    link.wait(s[3], full_high, up)


def ring_spread(link, me, up, down, piece, half):
    s = [link.slot() for _ in range(4)]
    mine = piece(me)
    link.start(s[0], mine, mine, up)
    link.start(s[1], mine, mine, down)
    yield
    low, high = piece(lax.rem(me + 3, 4)), piece(lax.rem(me + 1, 4))
    link.wait(s[0], low, down)
    link.start(s[2], half(low, 0), half(low, 0), up)
    link.wait(s[1], high, up)
    link.start(s[3], half(high, 1), half(high, 1), down)
    yield
    far = piece(lax.rem(me + 2, 4))
    link.wait(s[2], half(far, 0), down)
    link.wait(s[3], half(far, 1), up)


def finish(steps):
    for _ in steps:
        pass


def greet(others):
    barrier = pltpu.get_barrier_semaphore()
    for other in others:
        pl.semaphore_signal(barrier, inc=1, device_id=other, device_id_type=MESH_ID)
    pl.semaphore_wait(barrier, len(others))


def cut_at(n, lower):
    return n // 32 * 16 if lower else n - n // 32 * 16


def cut(n, lower):
    at = cut_at(n, lower)
    return lambda ref, i: ref.at[pl.ds(0, at) if i == 0 else pl.ds(at, n - at)]


LOW_FRONT = 64
LOW_BACK = 80


def rows_chain(r, link, p):
    core, y, xh = p.core, p.y, p.xh
    sib, across = device(core=1 - core), device(xh=1 - xh)
    up, down = device(y=lax.rem(y + 1, 4)), device(y=lax.rem(y + 3, 4))
    near = y + 1 - 2 * lax.rem(y, 2)
    pair = device(y=near)
    gq, gkv, sib_kv, cat = r.gq, r.gkv, r.sib_kv, r.cat
    sib_q = cat.at[:, :, pl.ds(2 * HD, 2 * HD)]
    one, two = link.slot(), link.slot()
    link.start(one, gkv.at[:, 1 - core], sib_kv, sib)
    link.start(two, gq.at[:, 1 - core], sib_q, sib)
    yield
    link.wait(one, sib_kv, sib)
    added(sib_kv, gkv.at[:, core])
    three = link.slot()
    odd = lax.rem(y, 2)
    half = HD // 2

    def columns(first):
        picks = [sib_kv[:, :, at + first : at + first + half] for at in (0, HD)]
        return jnp.concatenate(picks, axis=2)

    low, high_half = columns(0), columns(half)
    r.kv_out[...] = jnp.where(odd == 1, low, high_half)
    r.kv_keep[...] = jnp.where(odd == 1, high_half, low)
    link.start(three, r.kv_out, r.pair_kv, pair)
    link.wait(two, sib_q, sib)
    cat[:, :, : 2 * HD] = gq[:, core]
    cat[:, :, 4 * HD :] = sib_kv[...]
    rows = 4 * cat.shape[1]
    width = r.part.shape[3]
    step = 512
    scale = width ** (-0.5)

    def products(side):
        left = cat[pl.ds(side * 4, 4)].reshape(rows, 6 * HD)

        def body(c, _):
            at = pl.ds(pl.multiple_of(c * step, step), step)
            out = dotg(left[:, : 2 * HD], r.w_query[at, :], NT)
            out = out + dotg(left[:, 2 * HD : 4 * HD], r.w_other[at, :], NT)
            out = out + jnp.dot(left[:, 4 * HD :], r.w_head[:, at], preferred_element_type=F32)
            out = out * scale
            r.part[side, :, :, at] = out.astype(BF).reshape(4, rows // 4, step)
            return 0

        lax.fori_loop(0, width // step, body, 0)

    part = r.part
    high = part.shape[2] - LOW_BACK
    top, rest = pl.ds(0, LOW_BACK), pl.ds(LOW_BACK, high)

    def ring(side, rows_at, n, bufs):
        return ring_reduce(
            link, y, up, down, lambda q: part.at[side, q, rows_at], cut(n, rows_at is rest), *bufs
        )

    names = ("part_low", "part_high", "full_low", "full_high")

    def bufs(k):
        return [getattr(r, name + str(k)) for name in names]

    products(1 - xh)
    across_slots = [link.slot() for _ in range(4)]
    order = [lax.rem(y + i, 4) for i in (2, 1, 3, 0)]
    for i, q in enumerate(order):
        link.start(across_slots[i], part.at[1 - xh, q, rest], r.cross.at[q], across)
    far_ring = ring(1 - xh, top, LOW_BACK, bufs(0))
    next(far_ring)
    products(xh)
    near_ring = ring(xh, top, LOW_BACK, bufs(1))
    next(near_ring)
    yield
    link.wait(three, r.pair_kv, pair)
    total = (r.kv_keep[...].astype(F32) + r.pair_kv[...].astype(F32)).astype(BF)
    r.kv_all[:, core] = total
    four = link.slot()
    link.start(four, r.kv_all.at[:, core], r.kv_all.at[:, core], sib)
    next(far_ring)
    link.wait(four, r.kv_all.at[:, 1 - core], sib)
    yield
    next(near_ring)
    yield
    finish(far_ring)
    done = part.at[1 - xh, y, top]
    done[...] = (
        done[...].astype(F32)
        + r.full_low0[...].astype(F32)
        + r.full_high0[...].astype(F32)
    ).astype(BF)
    last = link.slot()
    link.start(last, done, r.cross_top, across)
    yield
    def crossed(i):
        link.wait(across_slots[i], r.cross.at[order[i]], across)
        added(part.at[xh, order[i], rest], r.cross.at[order[i]])

    crossed(0)
    rest_ring = ring(xh, rest, high, bufs(2))
    next(rest_ring)
    yield
    crossed(1)
    crossed(2)
    finish(near_ring)
    next(rest_ring)
    yield
    crossed(3)
    finish(rest_ring)
    link.wait(last, r.cross_top, across)
    own = part.at[xh, y]
    top_rows = (
        own[top].astype(F32)
        + r.full_low1[...].astype(F32)
        + r.full_high1[...].astype(F32)
        + r.cross_top[...].astype(F32)
    )
    rest_rows = (
        own[rest].astype(F32)
        + r.full_low2[...].astype(F32)
        + r.full_high2[...].astype(F32)
    )
    for first, grad_normed in ((0, top_rows), (LOW_BACK, rest_rows)):
        at = pl.ds(first, grad_normed.shape[0])
        inputs = r.tokens[at, :].astype(F32)
        reciprocal = lax.rsqrt(jnp.mean(inputs * inputs, axis=1, keepdims=True) + norm_eps)
        unit = inputs * reciprocal
        grad_unit = grad_normed * r.gain[...]
        inner = jnp.mean(grad_unit * unit, axis=1, keepdims=True)
        r.grad_tokens[at, :] = (reciprocal * (grad_unit - unit * inner)).astype(BF)


def weight_chain(r, link, p):
    core, y, xh, xl, z = p.core, p.y, p.xh, p.xl, p.z
    up, down = device(z=lax.rem(z + 1, 4)), device(z=lax.rem(z + 3, 4))
    beside = device(xl=1 - xl)
    wide = 2 * HD
    thin = HD // INNER
    length = r.turned.shape[1]
    share = r.rows.shape[2]
    width = 8 * share
    scale = width ** (-0.5)
    index = lambda ref, i: ref.at[i]
    chains = ("q", "kv")

    def ring(n):
        grad = getattr(r, n + "_grad")
        bufs = [getattr(r, n + end) for end in ("_low", "_high", "_full_low", "_full_high")]
        return ring_reduce(link, z, up, down, lambda q: grad.at[q], index, *bufs)

    r.turned[...] = r.gq[...].reshape(length, wide).T

    def query_part(c, _):
        r.arrive(c)
        out = jnp.dot(r.turned[...], r.rows[c], preferred_element_type=F32) * scale
        r.q_grad[lax.rem(c, 4), c // 4] = out.T.astype(BF)
        return 0

    lax.fori_loop(0, 8, query_part, 0)
    rings = {"q": ring("q")}
    next(rings["q"])
    yield
    next(rings["q"])
    yield
    which = pl.multiple_of(core * thin, thin)
    r.turned[:HD, :] = r.kv_all[...].reshape(length, HD).T
    r.kv_turned[:thin, :] = r.turned[pl.ds(which, thin), :]
    r.kv_turned[thin:, :] = r.turned[pl.ds(which + HD // 2, thin), :]

    def kv_part(c, _):
        out = jnp.dot(r.kv_turned[...], r.rows[c], preferred_element_type=F32) * scale
        r.kv_grad[lax.rem(c, 4), c // 4] = out.astype(BF)
        return 0

    lax.fori_loop(0, 8, kv_part, 0)
    rings["kv"] = ring("kv")
    next(rings["kv"])
    yield
    slots = {}
    for n in chains:
        if n == "kv":
            next(rings[n])
            yield
        finish(rings[n])
        mine = getattr(r, n + "_grad").at[z]
        for i in range(2):
            mine[i] = (
                mine[i].astype(F32)
                + getattr(r, n + "_full_low")[i].astype(F32)
                + getattr(r, n + "_full_high")[i].astype(F32)
            ).astype(BF)
        slots[n] = link.slot()
        link.start(slots[n], mine.at[1 - xl], getattr(r, n + "_beside"), beside)
        yield
    square = jnp.zeros((1, 1), F32)
    for n in chains:
        link.wait(slots[n], getattr(r, n + "_beside"), beside)
        summed = getattr(r, n + "_grad")[z, xl].astype(F32) + getattr(r, n + "_beside")[...].astype(F32)
        getattr(r, n + "_summed")[...] = summed
        part = jnp.sum(summed * summed, axis=0, keepdims=True)
        square = square + jnp.sum(part, axis=1, keepdims=True)
    x = xh * 2 + xl
    stages = (
        [device(core=1 - core)],
        [device(x=lax.rem(x + i, 4)) for i in (1, 2, 3)],
        [device(y=lax.rem(y + i, 4)) for i in (1, 2, 3)],
        [device(z=lax.rem(z + i, 4)) for i in (1, 2, 3)],
    )
    def place_of(q, side):
        return pl.ds(pl.multiple_of((side * 4 + q) * share, share), share)

    here = place_of(z, xl)
    r.fresh_q[here, :] = r.q_summed[...].astype(BF)
    r.fresh_kv[:, here] = r.kv_summed[...].astype(BF)
    views = dict(
        q=lambda q, side: r.fresh_q.at[place_of(q, side)],
        kv=lambda q, side: r.fresh_kv.at[:, place_of(q, side)],
    )
    cuts = dict(
        q=lambda ref, i: ref.at[pl.ds(i * share // 2, share // 2)],
        kv=lambda ref, i: ref.at[pl.ds(i * thin, thin)],
    )

    def spread(side):
        return [
            ring_spread(sums, z, up, down, functools.partial(views[n], side=side), cuts[n])
            for n in chains
        ]

    total = jnp.broadcast_to(square, (8, HD))
    sums = Link(r.send_sum, r.recv_sum)
    first, second = spread(xl), spread(1 - xl)
    for k, others in enumerate(stages):
        r.square[k] = total
        slot = [link.slot() for _ in others]
        for i, other in enumerate(others):
            link.start(slot[i], r.square.at[k], r.squares.at[k, i], other)
        if k == 0:
            for n in chains:
                slots[n] = sums.slot()
                sums.start(slots[n], views[n](z, xl), views[n](z, xl), beside)
            for ring_steps in first:
                next(ring_steps)
        if k == 2:
            for n in chains:
                sums.wait(slots[n], views[n](z, 1 - xl), beside)
            for ring_steps in second:
                next(ring_steps)
        if k == 3:
            for ring_steps in first:
                next(ring_steps)
        yield
        for i, other in enumerate(others):
            back = others[len(others) - 1 - i]
            link.wait(slot[i], r.squares.at[k, i], back)
            total = total + r.squares[k, i]
    for ring_steps in second:
        next(ring_steps)
    count_all = 1.0 * D * HD * (HEADS + 2 * KVH)
    factor = lax.rsqrt(total[:1, :1] / count_all + stat_eps)
    r.next_q[...] = keep_rate * r.moment_q[...] + r.q_summed[...] * factor
    r.next_kv[...] = keep_rate * r.moment_kv[...] + r.kv_summed[...] * factor
    few = r.fresh_kv.shape[0]

    def update(side):
        def body(q, _):
            at = place_of(q, side)
            moment = r.moment_all[side * 4 + q].astype(F32)
            moved = keep_rate * moment[:share] + r.fresh_q[at, :].astype(F32) * factor
            r.fresh_q[at, :] = (r.w_query[at, :].astype(F32) - learn_rate * moved).astype(BF)
            moment = jnp.concatenate([moment[share : share + few], moment[share + few :]], axis=1)
            moved = keep_rate * moment + r.fresh_kv[:, at].astype(F32) * factor
            r.fresh_kv[:, at] = (r.kv_own[:, at].astype(F32) - learn_rate * moved).astype(BF)
            return 0

        lax.fori_loop(0, 4, body, 0)

    yield
    for ring_steps in first:
        finish(ring_steps)
    yield
    for ring_steps in second:
        finish(ring_steps)
    sums.drain()
    update(xl)
    update(1 - xl)


def back_kernel(names, *refs):
    r = SimpleNamespace(**dict(zip(names, refs)))
    p = place()
    link = Link(r.send, r.recv)
    step = r.rows.shape[2]
    for c in range(8):
        pltpu.make_async_copy(
            r.rows_hbm.at[:, pl.ds(c * step, step)], r.rows.at[c], r.load.at[c]
        ).start()

    def arrive(c):
        pltpu.make_async_copy(
            r.rows_hbm.at[:, pl.ds(pl.multiple_of(c * step, step), step)], r.rows.at[c], r.load.at[c]
        ).wait()

    r.arrive = arrive
    x = p.xh * 2 + p.xl
    others = [device(core=1 - p.core)]
    for i in (1, 2, 3):
        others.append(device(x=lax.rem(x + i, 4)))
        others.append(device(y=lax.rem(p.y + i, 4)))
        others.append(device(z=lax.rem(p.z + i, 4)))
    greet(others)
    rows, weights = rows_chain(r, link, p), weight_chain(r, link, p)
    for which in ORDER:
        next(rows if which == "r" else weights, None)
    finish(rows)
    finish(weights)
    link.drain()


ORDER = "rwrwrwrwwwwwwwrrwwrw"


def back(
    gq, gkv, w_query, w_other, w_head, kv_own, tokens, gain, rows, moment_q, moment_kv, moment_all
):
    length, width = rows.shape
    share, wide = moment_q.shape
    few = moment_kv.shape[0]
    block = length // 16
    v = pltpu.VMEM
    shape = jax.ShapeDtypeStruct
    ins = dict(
        gq=gq,
        gkv=gkv,
        w_query=w_query,
        w_other=w_other,
        w_head=w_head,
        kv_own=kv_own,
        tokens=tokens,
        gain=gain,
        rows_hbm=rows,
        moment_q=moment_q,
        moment_kv=moment_kv,
        moment_all=moment_all,
    )
    outs = dict(
        grad_tokens=shape((block, width), BF),
        fresh_q=shape(w_query.shape, BF),
        fresh_kv=shape((few, width), BF),
        next_q=shape(moment_q.shape, F32),
        next_kv=shape(moment_kv.shape, F32),
    )
    scratch = dict(
        sib_kv=v((8, block, wide), BF),
        pair_kv=v((8, block, HD), BF),
        kv_out=v((8, block, HD), BF),
        kv_keep=v((8, block, HD), BF),
        kv_all=v((8, 2, block, HD), BF),
        cat=v((8, block, 3 * wide), BF),
        part=v((2, 4, block, width), BF),
        cross=v((4, block - LOW_BACK, width), BF),
        cross_top=v((LOW_BACK, width), BF),
        rows=v((8, length, share), BF),
        load=pltpu.SemaphoreType.DMA((8,)),
        turned=v((wide, length), BF),
        kv_turned=v((few, length), BF),
        send_sum=pltpu.SemaphoreType.DMA((20,)),
        recv_sum=pltpu.SemaphoreType.DMA((20,)),
        square=v((4, 8, HD), F32),
        squares=v((4, 3, 8, HD), F32),
        send=pltpu.SemaphoreType.DMA((64,)),
        recv=pltpu.SemaphoreType.DMA((64,)),
    )
    for k, n in enumerate((LOW_BACK, LOW_BACK, block - LOW_BACK)):
        first = cut_at(n, k == 2)
        scratch["part_low" + str(k)] = v((first, width), BF)
        scratch["part_high" + str(k)] = v((n - first, width), BF)
        scratch["full_low" + str(k)] = v((n, width), BF)
        scratch["full_high" + str(k)] = v((n, width), BF)
    for n, dims in (("q", (share, wide)), ("kv", (few, share))):
        scratch[n + "_grad"] = v((4, 2, *dims), BF)
        scratch[n + "_low"] = v(dims, BF)
        scratch[n + "_high"] = v(dims, BF)
        scratch[n + "_full_low"] = v((2, *dims), BF)
        scratch[n + "_full_high"] = v((2, *dims), BF)
        scratch[n + "_beside"] = v(dims, BF)
        scratch[n + "_summed"] = v(dims, F32)
    whole = pl.BlockSpec(memory_space=pltpu.VMEM)
    far = pl.BlockSpec(memory_space=pl.ANY)
    return pl.pallas_call(
        functools.partial(back_kernel, tuple(ins) + tuple(outs) + tuple(scratch)),
        in_specs=[far if n == "rows_hbm" else whole for n in ins],
        out_specs=[whole] * len(outs),
        out_shape=list(outs.values()),
        scratch_shapes=list(scratch.values()),
        compiler_params=pltpu.CompilerParams(
            collective_id=1, has_side_effects=True, vmem_limit_bytes=62 * 1024 * 1024
        ),
        name="back",
    )(*ins.values())

def front_kernel(names, *refs):
    r = SimpleNamespace(**dict(zip(names, refs)))
    p = place()
    link = Link(r.send, r.recv)
    core, y, xh = p.core, p.y, p.xh
    sib, across = device(core=1 - core), device(xh=1 - xh)
    up, down = device(y=lax.rem(y + 1, 4)), device(y=lax.rem(y + 3, 4))
    odd = lax.rem(y, 2)
    pair = device(y=y + 1 - 2 * odd)
    z = p.z
    z_up, z_down = device(z=lax.rem(z + 1, 4)), device(z=lax.rem(z + 3, 4))
    greet([sib, across, up, down, z_up, z_down])
    rows, kv = r.rows, r.kv
    block, width = rows.shape[3], rows.shape[4]
    thin = HD // INNER
    mine, other = odd * 2 + core, (1 - odd) * 2 + core
    kv_slots = [link.slot() for _ in range(4)]
    quarter = kv.shape[1] // 4

    def kv_piece(which):
        return lambda q: kv.at[which, pl.ds(pl.multiple_of(q * quarter, quarter), quarter)]

    kv[mine] = r.kv_own[...]
    link.start(kv_slots[0], kv_piece(mine)(z), kv_piece(mine)(z), pair)
    inputs = r.tokens[...].astype(F32)
    reciprocal = lax.rsqrt(jnp.mean(inputs * inputs, axis=1, keepdims=True) + norm_eps)
    rows[xh, y, core] = (inputs * reciprocal * r.gain[...]).astype(BF)
    top, rest = pl.ds(0, LOW_FRONT), pl.ds(LOW_FRONT, block - LOW_FRONT)

    def cross(slot, q, at):
        link.start(slot, rows.at[xh, q, core, at], rows.at[xh, q, core, at], across)

    def crossed(slot, q, at):
        link.wait(slot, rows.at[1 - xh, q, core, at], across)

    def to_sib(slot, side, q):
        link.start(slot, rows.at[side, q, core], rows.at[side, q, core], sib)

    def spread(side, at, n):
        return ring_spread(link, y, up, down, lambda q: rows.at[side, q, core, at], cut(n, at is rest))

    top_slot = link.slot()
    rest_slots = [link.slot() for _ in range(4)]
    sib_slots = [[link.slot() for _ in range(4)] for _ in range(2)]
    q0, q1, q2, q3 = y, lax.rem(y + 1, 4), lax.rem(y + 2, 4), lax.rem(y + 3, 4)
    cross(top_slot, q0, top)
    b_own = spread(xh, rest, block - LOW_FRONT)
    next(b_own)
    a_own = spread(xh, top, LOW_FRONT)
    next(a_own)
    cross(rest_slots[0], q0, rest)
    to_sib(sib_slots[0][0], xh, q0)
    link.start(kv_slots[1], kv.at[mine], kv.at[mine], sib)
    link.start(kv_slots[3], r.w_query, r.w_other, sib)
    stored = []

    def project(side, q, k):
        which = (0, 1, 2, 3)[k % 4]
        link.wait(sib_slots[k // 4][which], rows.at[side, q, 1 - core], sib)
        copy = pltpu.make_async_copy(rows.at[side, q], r.rows_out.at[side, q], r.store.at[k])
        copy.start()
        stored.append(copy)
        acc = r.acc
        acc[...] = jnp.zeros_like(acc)
        step = 512

        def body(c, _):
            at = pl.ds(pl.multiple_of(c * step, step), step)
            part = rows[side, q, :, :, at].reshape(2 * block, step)
            acc[:, : 2 * HD] += jnp.dot(part, r.w_query[at, :], preferred_element_type=F32)
            acc[:, 2 * HD :] += dotg(part, r.kv_out[:, at], NT)
            return 0

        lax.fori_loop(0, width // step, body, 0)
        scale = width ** (-0.5)
        here = pl.ds(pl.multiple_of((side * 4 + q) * 2 * block, 2 * block), 2 * block)
        cos, sin = r.cos[here, :], r.sin[here, :]
        for h in range(2):
            r.query[here, h * HD : (h + 1) * HD] = rope(
                acc[:, h * HD : (h + 1) * HD] * scale, cos, sin, 1.0
            ).astype(BF)
        r.key[here, :] = rope(acc[:, 2 * HD : 3 * HD] * scale, cos, sin, 1.0).astype(BF)
        r.value[here, :] = (acc[:, 3 * HD :] * scale).astype(BF)

    link.wait(kv_slots[0], kv_piece(other)(z), pair)
    sides = lambda ref, i: ref.at[:, pl.ds(i * (width // 2), width // 2)]
    kv_ring = ring_spread(link, z, z_up, z_down, kv_piece(other), sides)
    next(kv_ring)
    next(kv_ring)
    finish(kv_ring)
    link.start(kv_slots[2], kv.at[other], kv.at[other], sib)
    crossed(top_slot, q0, top)
    a_far = spread(1 - xh, top, LOW_FRONT)
    next(a_far)
    next(b_own)
    cross(rest_slots[1], q1, rest)
    cross(rest_slots[3], q3, rest)
    next(a_own)
    to_sib(sib_slots[0][1], xh, q1)
    to_sib(sib_slots[0][3], xh, q3)
    crossed(rest_slots[0], q0, rest)
    to_sib(sib_slots[1][0], 1 - xh, q0)
    finish(b_own)
    cross(rest_slots[2], q2, rest)
    finish(a_own)
    to_sib(sib_slots[0][2], xh, q2)
    next(a_far)
    link.wait(kv_slots[1], kv.at[odd * 2 + 1 - core], sib)
    link.wait(kv_slots[2], kv.at[(1 - odd) * 2 + 1 - core], sib)
    for j in range(INNER):
        r.kv_out[j * thin : (j + 1) * thin, :] = kv[j, :thin, :]
        r.kv_out[HD + j * thin : HD + (j + 1) * thin, :] = kv[j, thin:, :]
    project(xh, q0, 0)
    project(xh, q1, 1)
    project(xh, q3, 3)
    project(1 - xh, q0, 4)
    project(xh, q2, 2)
    finish(a_far)
    crossed(rest_slots[1], q1, rest)
    to_sib(sib_slots[1][1], 1 - xh, q1)
    crossed(rest_slots[3], q3, rest)
    to_sib(sib_slots[1][3], 1 - xh, q3)
    crossed(rest_slots[2], q2, rest)
    to_sib(sib_slots[1][2], 1 - xh, q2)
    project(1 - xh, q1, 5)
    project(1 - xh, q3, 7)
    project(1 - xh, q2, 6)
    link.wait(kv_slots[3], r.w_other, sib)
    for copy in stored:
        copy.wait()
    link.drain()


def front(tokens, gain, w_query, kv_own, cos, sin):
    block, width = tokens.shape
    length = cos.shape[0]
    v = pltpu.VMEM
    shape = jax.ShapeDtypeStruct
    ins = dict(tokens=tokens, gain=gain, w_query=w_query, kv_own=kv_own, cos=cos, sin=sin)
    outs = dict(
        query=shape((length, 2 * HD), BF),
        key=shape((length, HD), BF),
        value=shape((length, HD), BF),
        rows_out=shape((2, 4, 2, block, width), BF),
        w_other=shape(w_query.shape, BF),
        kv_out=shape((2 * HD, width), BF),
    )
    scratch = dict(
        rows=v((2, 4, 2, block, width), BF),
        kv=v((INNER, 2 * HD // INNER, width), BF),
        acc=v((2 * block, 4 * HD), F32),
        store=pltpu.SemaphoreType.DMA((8,)),
        send=pltpu.SemaphoreType.DMA((40,)),
        recv=pltpu.SemaphoreType.DMA((40,)),
    )
    whole = pl.BlockSpec(memory_space=pltpu.VMEM)
    far = pl.BlockSpec(memory_space=pl.ANY)
    return pl.pallas_call(
        functools.partial(front_kernel, tuple(ins) + tuple(outs) + tuple(scratch)),
        in_specs=[whole] * len(ins),
        out_specs=[whole, whole, whole, far, far, whole],
        out_shape=list(outs.values()),
        scratch_shapes=list(scratch.values()),
        compiler_params=pltpu.CompilerParams(
            collective_id=2, has_side_effects=True, vmem_limit_bytes=60 * 1024 * 1024
        ),
        name="front",
    )(*ins.values())


def tables(length):
    within = np.arange(HD) // 2
    rates = np.power(np.float32(rope_base), within.astype(np.float32) * np.float32(-2.0 / HD))
    angle = np.arange(length, dtype=np.float32)[:, None] * rates.astype(np.float32)[None, :]
    angle = angle.astype(np.float64)
    return np.cos(angle).astype(np.float32), np.sin(angle).astype(np.float32)


def per_device(
    tokens, cotangent, gain, w_query, w_key, w_value, moment_query, moment_key, moment_value
):
    key_width = w_key.shape[1]
    width = tokens.shape[2]
    cos, sin = tables(cotangent.shape[1])
    kv_own = jnp.concatenate([w_key, w_value], axis=1).T
    moment_kv = jnp.concatenate([moment_key, moment_value], axis=1).T
    halves = jnp.split(moment_kv, 2, axis=1)
    moment_own = jnp.concatenate([moment_query, *halves], axis=0).astype(BF)
    moment_all = lax.all_gather(moment_own, DP)
    query, key, value, rows, w_other, w_head = front(
        tokens[0], gain[None], w_query, kv_own, cos, sin
    )
    length = query.shape[0]
    rows = rows.reshape(length, width)
    attended, grad_query, grad_kv = attention(query, key, value, cotangent[0], cos, sin)
    by_block = (8, 2, length // 16, 2 * HD)
    grad_tokens, fresh_query, fresh_kv, next_query, next_kv = back(
        grad_query.reshape(by_block),
        grad_kv.reshape(by_block),
        w_query,
        w_other,
        w_head,
        kv_own,
        tokens[0],
        gain[None],
        rows,
        moment_query,
        moment_kv,
        moment_all,
    )
    fresh_key, fresh_value = fresh_kv[:key_width].T, fresh_kv[key_width:].T
    next_key, next_value = next_kv[:key_width].T, next_kv[key_width:].T
    return (
        attended[None],
        grad_tokens[None],
        fresh_query,
        fresh_key,
        fresh_value,
        next_query,
        next_key,
        next_value,
    )


def solution(mesh):
    torus = Mesh(mesh.devices.reshape(2, 4, 2, 2, 2, 2), ALL)
    placed = (
        P(DP, TENSOR, None),
        P(DP, None, TENSOR),
        P(),
        P(None, TENSOR),
        P(None, TENSOR),
        P(None, TENSOR),
        P(DP, TENSOR),
        P(DP, TENSOR),
        P(DP, TENSOR),
    )
    return jax.shard_map(
        per_device,
        mesh=torus,
        in_specs=placed,
        out_specs=(
            P(DP, None, TENSOR),
            P(DP, TENSOR, None),
            P(None, TENSOR),
            P(None, TENSOR),
            P(None, TENSOR),
            P(DP, TENSOR),
            P(DP, TENSOR),
            P(DP, TENSOR),
        ),
        check_vma=False,
    )
```

```python
import functools
from types import SimpleNamespace

import jax
import jax.numpy as jnp
import numpy as np
from jax import lax
from jax.experimental import pallas as pl
from jax.experimental.pallas import tpu as pltpu
from jax.sharding import Mesh
from jax.sharding import PartitionSpec as P

D = 4096
HEADS = 32
KVH = 4
HD = 128
F32 = jnp.float32
BF = jnp.bfloat16
CHIPS = ("x", "yh", "yl")
TENSOR = ("x", "yh", "yl", "core")
SHARE = ("yl", "core")
DP = ("dp_0", "dp_1")
ALL = ("dp_0", "dp_1", "x", "yh", "yl", "core")

rope_base = 1000000.0
norm_eps = 1e-06
stat_eps = 1e-06
learn_rate = 0.05
keep_rate = 0.9


def rope(x, cos, sin, sign):
    lane = lax.broadcasted_iota(jnp.int32, x.shape, 1)
    nxt = pltpu.roll(x, x.shape[1]-1, 1)
    prv = pltpu.roll(x, 1, 1)
    partner = jnp.where(lane % 2 == 0, -nxt, prv)
    return x*cos + partner*(sin*sign)

NT=(((1,),(1,)),((),()))
TN=(((0,),(0,)),((),()))
def dotg(a,b,dims):
    return lax.dot_general(a,b,dims,preferred_element_type=F32)

def attn_kernel(BQ, TC, hs, q_ref, k_ref, v_ref, do_ref, cos_ref, sin_ref,
                out_ref, gq_ref, gkv_ref, va, s_scr, r_scr, p_scr, dk, dv, m_scr, o_scr, g_scr):
    i = pl.program_id(0)
    n = pl.num_programs(0)
    T = k_ref.shape[0]
    R = 2*BQ
    @pl.when(i == 0)
    def _():
        va[:, :HD] = v_ref[...]
        va[:, HD:] = jnp.ones((T, HD), BF)
        dk[...] = jnp.zeros_like(dk)
        dv[...] = jnp.zeros_like(dv)
    q = jnp.concatenate([q_ref[:, :HD], q_ref[:, HD:]], axis=0)
    do = jnp.concatenate([do_ref[:, :HD], do_ref[:, HD:]], axis=0)
    first = i*BQ
    full = first // TC
    used = (first + BQ + TC - 1)//TC
    m_scr[...] = jnp.full((R, HD), -3e38, F32)
    def lane_max(s):
        m = m_scr[...]
        for j in range(TC//HD):
            m = jnp.maximum(m, s[:, j*HD:(j+1)*HD])
        m_scr[...] = m
    def scores(c):
        ks = k_ref[pl.ds(pl.multiple_of(c*TC, TC), TC), :]
        vs = v_ref[pl.ds(pl.multiple_of(c*TC, TC), TC), :]
        r_scr[c] = dotg(do, vs, NT)
        return dotg(q, ks, NT)
    def body1(c, _):
        s = scores(c)
        s_scr[c] = s
        lane_max(s)
        return 0
    lax.fori_loop(0, full, body1, 0)
    def body1d(c, _):
        s = scores(c)
        row = first + lax.broadcasted_iota(jnp.int32, (R, TC), 0) % BQ
        col = c*TC + lax.broadcasted_iota(jnp.int32, (R, TC), 1)
        s = jnp.where(row >= col, s, -1e30)
        s_scr[c] = s
        lane_max(s)
        return 0
    lax.fori_loop(full, used, body1d, 0)
    c2 = hs * 1.4426950408889634
    m = jnp.max(m_scr[...], axis=1, keepdims=True)
    mb = jnp.broadcast_to(m * c2, (R, HD))
    o_scr[...] = jnp.zeros_like(o_scr)
    def body2(c, _):
        s = s_scr[c]
        p = jnp.concatenate([jnp.exp2(s[:, j*HD:(j+1)*HD]*c2 - mb) for j in range(TC//HD)], axis=1).astype(BF)
        p_scr[c] = p
        o_scr[...] += jnp.dot(p, va[pl.ds(pl.multiple_of(c*TC, TC), TC), :], preferred_element_type=F32)
        return 0
    lax.fori_loop(0, used, body2, 0)
    inv = 1.0 / o_scr[:, HD:]
    o = o_scr[:, :HD] * inv
    out_ref[:, :HD] = o[:BQ].astype(BF)
    out_ref[:, HD:] = o[BQ:].astype(BF)
    dof = do.astype(F32)
    delta = jnp.broadcast_to(jnp.sum(dof*o, axis=1, keepdims=True), (R, HD))
    qn = (q.astype(F32) * (inv*hs)).astype(BF)
    don = (dof*inv).astype(BF)
    g_scr[...] = jnp.zeros_like(g_scr)
    def body3(c, _):
        at = pl.ds(pl.multiple_of(c*TC, TC), TC)
        p = p_scr[c]
        r = r_scr[c]
        pf = p.astype(F32)
        g = jnp.concatenate([pf[:, j*HD:(j+1)*HD]*(r[:, j*HD:(j+1)*HD] - delta) for j in range(TC//HD)], axis=1).astype(BF)
        g_scr[...] += jnp.dot(g, k_ref[at, :], preferred_element_type=F32)
        dk[at, :] += dotg(g, qn, TN)
        dv[at, :] += dotg(p, don, TN)
        return 0
    lax.fori_loop(0, used, body3, 0)
    gq = g_scr[...] * (inv*hs)
    here = pl.ds(pl.multiple_of(first, BQ), BQ)
    cos = cos_ref[here, :]
    sin = sin_ref[here, :]
    gq_ref[:, :HD] = rope(gq[:BQ], cos, sin, -1.0).astype(BF)
    gq_ref[:, HD:] = rope(gq[BQ:], cos, sin, -1.0).astype(BF)
    @pl.when(i == n-1)
    def _():
        gkv_ref[:, :HD] = rope(dk[...], cos_ref[...], sin_ref[...], -1.0).astype(BF)
        gkv_ref[:, HD:] = dv[...].astype(BF)

def attention(q, k, v, do, cos, sin, BQ=512, TC=512):
    T = q.shape[0]
    R = 2*BQ
    whole = pl.BlockSpec((T, HD), lambda i: (0, 0))
    rows = pl.BlockSpec((BQ, 2*HD), lambda i: (i, 0))
    return pl.pallas_call(
        functools.partial(attn_kernel, BQ, TC, HD**-0.5),
        grid=(T//BQ,),
        in_specs=[rows, whole, whole, rows, whole, whole],
        out_specs=[rows, rows, pl.BlockSpec((T, 2*HD), lambda i: (0, 0))],
        out_shape=[jax.ShapeDtypeStruct((T, 2*HD), BF)]*3,
        scratch_shapes=[pltpu.VMEM((T, 2*HD), BF), pltpu.VMEM((T//TC, R, TC), F32), pltpu.VMEM((T//TC, R, TC), F32),
            pltpu.VMEM((T//TC, R, TC), BF), pltpu.VMEM((T, HD), F32), pltpu.VMEM((T, HD), F32),
            pltpu.VMEM((R, HD), F32), pltpu.VMEM((R, 2*HD), F32), pltpu.VMEM((R, HD), F32)],
        compiler_params=pltpu.CompilerParams(vmem_limit_bytes=56*1024*1024),
        name="attention",
    )(q, k, v, do, cos, sin)


MESH_ID = pl.DeviceIdType.MESH
INNER = 4


def place():
    at = lax.axis_index
    return SimpleNamespace(
        xl=at("dp_0"), z=at("dp_1"), xh=at("x"), y=at("yh") * 2 + at("yl"), core=at("core")
    )


def device(**moved):
    names = {}
    for key, value in moved.items():
        if key == "y":
            names["yh"] = value // 2
            names["yl"] = value % 2
        elif key == "x":
            names["x"] = value // 2
            names["dp_0"] = value % 2
        else:
            names[{"xl": "dp_0", "z": "dp_1", "xh": "x", "core": "core"}[key]] = value
    return names


class Link:
    def __init__(self, send, recv):
        self.send, self.recv, self.used, self.sent = send, recv, 0, []

    def slot(self):
        self.used += 1
        return self.used - 1

    def start(self, slot, src, dst, to):
        copy = pltpu.make_async_remote_copy(
            src_ref=src,
            dst_ref=dst,
            send_sem=self.send.at[slot],
            recv_sem=self.recv.at[slot],
            device_id=to,
            device_id_type=MESH_ID,
        )
        copy.start()
        self.sent.append(copy)

    def wait(self, slot, landed, to):
        pltpu.make_async_remote_copy(
            src_ref=landed,
            dst_ref=landed,
            send_sem=self.send.at[slot],
            recv_sem=self.recv.at[slot],
            device_id=to,
            device_id_type=MESH_ID,
        ).wait_recv()

    def drain(self):
        for copy in self.sent:
            copy.wait_send()


def added(ref, other):
    ref[...] = (ref[...].astype(F32) + other[...].astype(F32)).astype(BF)


def ring_reduce(link, me, up, down, piece, half, part_low, part_high, full_low, full_high):
    s = [link.slot() for _ in range(4)]
    far = piece(lax.rem(me + 2, 4))
    link.start(s[0], half(far, 0), part_low, up)
    link.start(s[1], half(far, 1), part_high, down)
    yield
    above = piece(lax.rem(me + 1, 4))
    link.wait(s[0], part_low, down)
    added(half(above, 0), part_low)
    link.start(s[2], above, full_low, up)
    below = piece(lax.rem(me + 3, 4))
    link.wait(s[1], part_high, up)
    added(half(below, 1), part_high)
    link.start(s[3], below, full_high, down)
    yield
    link.wait(s[2], full_low, down)
    link.wait(s[3], full_high, up)


def ring_spread(link, me, up, down, piece, half):
    s = [link.slot() for _ in range(4)]
    mine = piece(me)
    link.start(s[0], mine, mine, up)
    link.start(s[1], mine, mine, down)
    yield
    low, high = piece(lax.rem(me + 3, 4)), piece(lax.rem(me + 1, 4))
    link.wait(s[0], low, down)
    link.start(s[2], half(low, 0), half(low, 0), up)
    link.wait(s[1], high, up)
    link.start(s[3], half(high, 1), half(high, 1), down)
    yield
    far = piece(lax.rem(me + 2, 4))
    link.wait(s[2], half(far, 0), down)
    link.wait(s[3], half(far, 1), up)


def finish(steps):
    for _ in steps:
        pass


def greet(others):
    barrier = pltpu.get_barrier_semaphore()
    for other in others:
        pl.semaphore_signal(barrier, inc=1, device_id=other, device_id_type=MESH_ID)
    pl.semaphore_wait(barrier, len(others))


def cut_at(n, lower):
    return n // 32 * 16 if lower else n - n // 32 * 16


def cut(n, lower):
    at = cut_at(n, lower)
    return lambda ref, i: ref.at[pl.ds(0, at) if i == 0 else pl.ds(at, n - at)]


LOW_FRONT = 64
LOW_BACK = 80


def rows_chain(r, link, p):
    core, y, xh = p.core, p.y, p.xh
    sib, across = device(core=1 - core), device(xh=1 - xh)
    up, down = device(y=lax.rem(y + 1, 4)), device(y=lax.rem(y + 3, 4))
    near = y + 1 - 2 * lax.rem(y, 2)
    pair = device(y=near)
    gq, gkv, sib_kv, cat = r.gq, r.gkv, r.sib_kv, r.cat
    sib_q = cat.at[:, :, pl.ds(2 * HD, 2 * HD)]
    one, two = link.slot(), link.slot()
    link.start(one, gkv.at[:, 1 - core], sib_kv, sib)
    link.start(two, gq.at[:, 1 - core], sib_q, sib)
    yield
    link.wait(one, sib_kv, sib)
    added(sib_kv, gkv.at[:, core])
    three = link.slot()
    odd = lax.rem(y, 2)
    half = HD // 2

    def columns(first):
        picks = [sib_kv[:, :, at + first : at + first + half] for at in (0, HD)]
        return jnp.concatenate(picks, axis=2)

    low, high_half = columns(0), columns(half)
    r.kv_out[...] = jnp.where(odd == 1, low, high_half)
    r.kv_keep[...] = jnp.where(odd == 1, high_half, low)
    link.start(three, r.kv_out, r.pair_kv, pair)
    link.wait(two, sib_q, sib)
    cat[:, :, : 2 * HD] = gq[:, core]
    cat[:, :, 4 * HD :] = sib_kv[...]
    rows = 4 * cat.shape[1]
    width = r.part.shape[3]
    step = 512
    scale = width ** (-0.5)

    def products(side):
        left = cat[pl.ds(side * 4, 4)].reshape(rows, 6 * HD)

        def body(c, _):
            at = pl.ds(pl.multiple_of(c * step, step), step)
            out = dotg(left[:, : 2 * HD], r.w_query[at, :], NT)
            out = out + dotg(left[:, 2 * HD : 4 * HD], r.w_other[at, :], NT)
            out = out + jnp.dot(left[:, 4 * HD :], r.w_head[:, at], preferred_element_type=F32)
            out = out * scale
            r.part[side, :, :, at] = out.astype(BF).reshape(4, rows // 4, step)
            return 0

        lax.fori_loop(0, width // step, body, 0)

    part = r.part
    high = part.shape[2] - LOW_BACK
    top, rest = pl.ds(0, LOW_BACK), pl.ds(LOW_BACK, high)

    def ring(side, rows_at, n, bufs):
        return ring_reduce(
            link, y, up, down, lambda q: part.at[side, q, rows_at], cut(n, rows_at is rest), *bufs
        )

    names = ("part_low", "part_high", "full_low", "full_high")

    def bufs(k):
        return [getattr(r, name + str(k)) for name in names]

    products(1 - xh)
    across_slots = [link.slot() for _ in range(4)]
    order = [lax.rem(y + i, 4) for i in (2, 1, 3, 0)]
    for i, q in enumerate(order):
        link.start(across_slots[i], part.at[1 - xh, q, rest], r.cross.at[q], across)
    far_ring = ring(1 - xh, top, LOW_BACK, bufs(0))
    next(far_ring)
    products(xh)
    near_ring = ring(xh, top, LOW_BACK, bufs(1))
    next(near_ring)
    yield
    link.wait(three, r.pair_kv, pair)
    total = (r.kv_keep[...].astype(F32) + r.pair_kv[...].astype(F32)).astype(BF)
    r.kv_all[:, core] = total
    four = link.slot()
    link.start(four, r.kv_all.at[:, core], r.kv_all.at[:, core], sib)
    next(far_ring)
    link.wait(four, r.kv_all.at[:, 1 - core], sib)
    yield
    next(near_ring)
    yield
    finish(far_ring)
    done = part.at[1 - xh, y, top]
    done[...] = (
        done[...].astype(F32)
        + r.full_low0[...].astype(F32)
        + r.full_high0[...].astype(F32)
    ).astype(BF)
    last = link.slot()
    link.start(last, done, r.cross_top, across)
    yield
    def crossed(i):
        link.wait(across_slots[i], r.cross.at[order[i]], across)
        added(part.at[xh, order[i], rest], r.cross.at[order[i]])

    crossed(0)
    rest_ring = ring(xh, rest, high, bufs(2))
    next(rest_ring)
    yield
    crossed(1)
    crossed(2)
    finish(near_ring)
    next(rest_ring)
    yield
    crossed(3)
    finish(rest_ring)
    link.wait(last, r.cross_top, across)
    own = part.at[xh, y]
    top_rows = (
        own[top].astype(F32)
        + r.full_low1[...].astype(F32)
        + r.full_high1[...].astype(F32)
        + r.cross_top[...].astype(F32)
    )
    rest_rows = (
        own[rest].astype(F32)
        + r.full_low2[...].astype(F32)
        + r.full_high2[...].astype(F32)
    )
    for first, grad_normed in ((0, top_rows), (LOW_BACK, rest_rows)):
        at = pl.ds(first, grad_normed.shape[0])
        inputs = r.tokens[at, :].astype(F32)
        reciprocal = lax.rsqrt(jnp.mean(inputs * inputs, axis=1, keepdims=True) + norm_eps)
        unit = inputs * reciprocal
        grad_unit = grad_normed * r.gain[...]
        inner = jnp.mean(grad_unit * unit, axis=1, keepdims=True)
        r.grad_tokens[at, :] = (reciprocal * (grad_unit - unit * inner)).astype(BF)


def weight_chain(r, link, p):
    core, y, xh, xl, z = p.core, p.y, p.xh, p.xl, p.z
    up, down = device(z=lax.rem(z + 1, 4)), device(z=lax.rem(z + 3, 4))
    beside = device(xl=1 - xl)
    wide = 2 * HD
    thin = HD // INNER
    length = r.turned.shape[1]
    share = r.rows.shape[2]
    width = 8 * share
    scale = width ** (-0.5)
    index = lambda ref, i: ref.at[i]
    chains = ("q", "kv")

    def ring(n):
        grad = getattr(r, n + "_grad")
        bufs = [getattr(r, n + end) for end in ("_low", "_high", "_full_low", "_full_high")]
        return ring_reduce(link, z, up, down, lambda q: grad.at[q], index, *bufs)

    r.turned[...] = r.gq[...].reshape(length, wide).T

    def query_part(c, _):
        r.arrive(c)
        out = jnp.dot(r.turned[...], r.rows[c], preferred_element_type=F32) * scale
        r.q_grad[lax.rem(c, 4), c // 4] = out.T.astype(BF)
        return 0

    lax.fori_loop(0, 8, query_part, 0)
    rings = {"q": ring("q")}
    next(rings["q"])
    yield
    next(rings["q"])
    yield
    which = pl.multiple_of(core * thin, thin)
    r.turned[:HD, :] = r.kv_all[...].reshape(length, HD).T
    r.kv_turned[:thin, :] = r.turned[pl.ds(which, thin), :]
    r.kv_turned[thin:, :] = r.turned[pl.ds(which + HD // 2, thin), :]

    def kv_part(c, _):
        out = jnp.dot(r.kv_turned[...], r.rows[c], preferred_element_type=F32) * scale
        r.kv_grad[lax.rem(c, 4), c // 4] = out.astype(BF)
        return 0

    lax.fori_loop(0, 8, kv_part, 0)
    rings["kv"] = ring("kv")
    next(rings["kv"])
    yield
    slots = {}
    for n in chains:
        if n == "kv":
            next(rings[n])
            yield
        finish(rings[n])
        mine = getattr(r, n + "_grad").at[z]
        for i in range(2):
            mine[i] = (
                mine[i].astype(F32)
                + getattr(r, n + "_full_low")[i].astype(F32)
                + getattr(r, n + "_full_high")[i].astype(F32)
            ).astype(BF)
        slots[n] = link.slot()
        link.start(slots[n], mine.at[1 - xl], getattr(r, n + "_beside"), beside)
        yield
    square = jnp.zeros((1, 1), F32)
    for n in chains:
        link.wait(slots[n], getattr(r, n + "_beside"), beside)
        summed = getattr(r, n + "_grad")[z, xl].astype(F32) + getattr(r, n + "_beside")[...].astype(F32)
        getattr(r, n + "_summed")[...] = summed
        part = jnp.sum(summed * summed, axis=0, keepdims=True)
        square = square + jnp.sum(part, axis=1, keepdims=True)
    x = xh * 2 + xl
    stages = (
        [device(core=1 - core)],
        [device(x=lax.rem(x + i, 4)) for i in (1, 2, 3)],
        [device(y=lax.rem(y + i, 4)) for i in (1, 2, 3)],
        [device(z=lax.rem(z + i, 4)) for i in (1, 2, 3)],
    )
    def place_of(q, side):
        return pl.ds(pl.multiple_of((side * 4 + q) * share, share), share)

    here = place_of(z, xl)
    r.fresh_q[here, :] = r.q_summed[...].astype(BF)
    r.fresh_kv[:, here] = r.kv_summed[...].astype(BF)
    views = dict(
        q=lambda q, side: r.fresh_q.at[place_of(q, side)],
        kv=lambda q, side: r.fresh_kv.at[:, place_of(q, side)],
    )
    cuts = dict(
        q=lambda ref, i: ref.at[pl.ds(i * share // 2, share // 2)],
        kv=lambda ref, i: ref.at[pl.ds(i * thin, thin)],
    )

    def spread(side):
        return [
            ring_spread(sums, z, up, down, functools.partial(views[n], side=side), cuts[n])
            for n in chains
        ]

    total = jnp.broadcast_to(square, (8, HD))
    sums = Link(r.send_sum, r.recv_sum)
    first, second = spread(xl), spread(1 - xl)
    for k, others in enumerate(stages):
        r.square[k] = total
        slot = [link.slot() for _ in others]
        for i, other in enumerate(others):
            link.start(slot[i], r.square.at[k], r.squares.at[k, i], other)
        if k == 0:
            for n in chains:
                slots[n] = sums.slot()
                sums.start(slots[n], views[n](z, xl), views[n](z, xl), beside)
            for ring_steps in first:
                next(ring_steps)
        if k == 2:
            for n in chains:
                sums.wait(slots[n], views[n](z, 1 - xl), beside)
            for ring_steps in second:
                next(ring_steps)
        if k == 3:
            for ring_steps in first:
                next(ring_steps)
        yield
        for i, other in enumerate(others):
            back = others[len(others) - 1 - i]
            link.wait(slot[i], r.squares.at[k, i], back)
            total = total + r.squares[k, i]
    for ring_steps in second:
        next(ring_steps)
    count_all = 1.0 * D * HD * (HEADS + 2 * KVH)
    factor = lax.rsqrt(total[:1, :1] / count_all + stat_eps)
    r.next_q[...] = keep_rate * r.moment_q[...] + r.q_summed[...] * factor
    r.next_kv[...] = keep_rate * r.moment_kv[...] + r.kv_summed[...] * factor
    few = r.fresh_kv.shape[0]

    def update(side):
        def body(q, _):
            at = place_of(q, side)
            moment = r.moment_all[side * 4 + q].astype(F32)
            moved = keep_rate * moment[:share] + r.fresh_q[at, :].astype(F32) * factor
            r.fresh_q[at, :] = (r.w_query[at, :].astype(F32) - learn_rate * moved).astype(BF)
            moment = jnp.concatenate([moment[share : share + few], moment[share + few :]], axis=1)
            moved = keep_rate * moment + r.fresh_kv[:, at].astype(F32) * factor
            r.fresh_kv[:, at] = (r.kv_own[:, at].astype(F32) - learn_rate * moved).astype(BF)
            return 0

        lax.fori_loop(0, 4, body, 0)

    yield
    for ring_steps in first:
        finish(ring_steps)
    yield
    for ring_steps in second:
        finish(ring_steps)
    sums.drain()
    update(xl)
    update(1 - xl)


def back_kernel(names, *refs):
    r = SimpleNamespace(**dict(zip(names, refs)))
    p = place()
    link = Link(r.send, r.recv)
    step = r.rows.shape[2]
    for c in range(8):
        pltpu.make_async_copy(
            r.rows_hbm.at[:, pl.ds(c * step, step)], r.rows.at[c], r.load.at[c]
        ).start()

    def arrive(c):
        pltpu.make_async_copy(
            r.rows_hbm.at[:, pl.ds(pl.multiple_of(c * step, step), step)], r.rows.at[c], r.load.at[c]
        ).wait()

    r.arrive = arrive
    x = p.xh * 2 + p.xl
    others = [device(core=1 - p.core)]
    for i in (1, 2, 3):
        others.append(device(x=lax.rem(x + i, 4)))
        others.append(device(y=lax.rem(p.y + i, 4)))
        others.append(device(z=lax.rem(p.z + i, 4)))
    greet(others)
    rows, weights = rows_chain(r, link, p), weight_chain(r, link, p)
    for which in ORDER:
        next(rows if which == "r" else weights, None)
    finish(rows)
    finish(weights)
    link.drain()


ORDER = "rwrwrwrwwwwwwwrrwwrw"


def back(
    gq, gkv, w_query, w_other, w_head, kv_own, tokens, gain, rows, moment_q, moment_kv, moment_all
):
    length, width = rows.shape
    share, wide = moment_q.shape
    few = moment_kv.shape[0]
    block = length // 16
    v = pltpu.VMEM
    shape = jax.ShapeDtypeStruct
    ins = dict(
        gq=gq,
        gkv=gkv,
        w_query=w_query,
        w_other=w_other,
        w_head=w_head,
        kv_own=kv_own,
        tokens=tokens,
        gain=gain,
        rows_hbm=rows,
        moment_q=moment_q,
        moment_kv=moment_kv,
        moment_all=moment_all,
    )
    outs = dict(
        grad_tokens=shape((block, width), BF),
        fresh_q=shape(w_query.shape, BF),
        fresh_kv=shape((few, width), BF),
        next_q=shape(moment_q.shape, F32),
        next_kv=shape(moment_kv.shape, F32),
    )
    scratch = dict(
        sib_kv=v((8, block, wide), BF),
        pair_kv=v((8, block, HD), BF),
        kv_out=v((8, block, HD), BF),
        kv_keep=v((8, block, HD), BF),
        kv_all=v((8, 2, block, HD), BF),
        cat=v((8, block, 3 * wide), BF),
        part=v((2, 4, block, width), BF),
        cross=v((4, block - LOW_BACK, width), BF),
        cross_top=v((LOW_BACK, width), BF),
        rows=v((8, length, share), BF),
        load=pltpu.SemaphoreType.DMA((8,)),
        turned=v((wide, length), BF),
        kv_turned=v((few, length), BF),
        send_sum=pltpu.SemaphoreType.DMA((20,)),
        recv_sum=pltpu.SemaphoreType.DMA((20,)),
        square=v((4, 8, HD), F32),
        squares=v((4, 3, 8, HD), F32),
        send=pltpu.SemaphoreType.DMA((64,)),
        recv=pltpu.SemaphoreType.DMA((64,)),
    )
    for k, n in enumerate((LOW_BACK, LOW_BACK, block - LOW_BACK)):
        first = cut_at(n, k == 2)
        scratch["part_low" + str(k)] = v((first, width), BF)
        scratch["part_high" + str(k)] = v((n - first, width), BF)
        scratch["full_low" + str(k)] = v((n, width), BF)
        scratch["full_high" + str(k)] = v((n, width), BF)
    for n, dims in (("q", (share, wide)), ("kv", (few, share))):
        scratch[n + "_grad"] = v((4, 2, *dims), BF)
        scratch[n + "_low"] = v(dims, BF)
        scratch[n + "_high"] = v(dims, BF)
        scratch[n + "_full_low"] = v((2, *dims), BF)
        scratch[n + "_full_high"] = v((2, *dims), BF)
        scratch[n + "_beside"] = v(dims, BF)
        scratch[n + "_summed"] = v(dims, F32)
    whole = pl.BlockSpec(memory_space=pltpu.VMEM)
    far = pl.BlockSpec(memory_space=pl.ANY)
    return pl.pallas_call(
        functools.partial(back_kernel, tuple(ins) + tuple(outs) + tuple(scratch)),
        in_specs=[far if n == "rows_hbm" else whole for n in ins],
        out_specs=[whole] * len(outs),
        out_shape=list(outs.values()),
        scratch_shapes=list(scratch.values()),
        compiler_params=pltpu.CompilerParams(
            collective_id=1, has_side_effects=True, vmem_limit_bytes=62 * 1024 * 1024
        ),
        name="back",
    )(*ins.values())

def front_kernel(names, *refs):
    r = SimpleNamespace(**dict(zip(names, refs)))
    p = place()
    link = Link(r.send, r.recv)
    core, y, xh = p.core, p.y, p.xh
    sib, across = device(core=1 - core), device(xh=1 - xh)
    up, down = device(y=lax.rem(y + 1, 4)), device(y=lax.rem(y + 3, 4))
    odd = lax.rem(y, 2)
    pair = device(y=y + 1 - 2 * odd)
    z = p.z
    z_up, z_down = device(z=lax.rem(z + 1, 4)), device(z=lax.rem(z + 3, 4))
    xl = p.xl
    beside = device(xl=1 - xl)
    greet([sib, across, up, down, z_up, z_down, beside])
    moments = r.moment_all
    here = moments.at[xl * 4 + z]
    placed = pltpu.make_async_copy(r.moment_own, here, r.store.at[8])
    placed.start()
    rows, kv = r.rows, r.kv
    block, width = rows.shape[3], rows.shape[4]
    thin = HD // INNER
    mine, other = odd * 2 + core, (1 - odd) * 2 + core
    kv_slots = [link.slot() for _ in range(4)]
    quarter = kv.shape[1] // 4

    def kv_piece(which):
        return lambda q: kv.at[which, pl.ds(pl.multiple_of(q * quarter, quarter), quarter)]

    kv[mine] = r.kv_own[...]
    link.start(kv_slots[0], kv_piece(mine)(z), kv_piece(mine)(z), pair)
    inputs = r.tokens[...].astype(F32)
    reciprocal = lax.rsqrt(jnp.mean(inputs * inputs, axis=1, keepdims=True) + norm_eps)
    rows[xh, y, core] = (inputs * reciprocal * r.gain[...]).astype(BF)
    top, rest = pl.ds(0, LOW_FRONT), pl.ds(LOW_FRONT, block - LOW_FRONT)

    def cross(slot, q, at):
        link.start(slot, rows.at[xh, q, core, at], rows.at[xh, q, core, at], across)

    def crossed(slot, q, at):
        link.wait(slot, rows.at[1 - xh, q, core, at], across)

    def to_sib(slot, side, q):
        link.start(slot, rows.at[side, q, core], rows.at[side, q, core], sib)

    def spread(side, at, n):
        return ring_spread(link, y, up, down, lambda q: rows.at[side, q, core, at], cut(n, at is rest))

    top_slot = link.slot()
    rest_slots = [link.slot() for _ in range(4)]
    sib_slots = [[link.slot() for _ in range(4)] for _ in range(2)]
    q0, q1, q2, q3 = y, lax.rem(y + 1, 4), lax.rem(y + 2, 4), lax.rem(y + 3, 4)
    cross(top_slot, q0, top)
    b_own = spread(xh, rest, block - LOW_FRONT)
    next(b_own)
    a_own = spread(xh, top, LOW_FRONT)
    next(a_own)
    cross(rest_slots[0], q0, rest)
    to_sib(sib_slots[0][0], xh, q0)
    link.start(kv_slots[1], kv.at[mine], kv.at[mine], sib)
    link.start(kv_slots[3], r.w_query, r.w_other, sib)
    stored = []

    def project(side, q, k):
        which = (0, 1, 2, 3)[k % 4]
        link.wait(sib_slots[k // 4][which], rows.at[side, q, 1 - core], sib)
        copy = pltpu.make_async_copy(rows.at[side, q], r.rows_out.at[side, q], r.store.at[k])
        copy.start()
        stored.append(copy)
        acc = r.acc
        acc[...] = jnp.zeros_like(acc)
        step = 512

        def body(c, _):
            at = pl.ds(pl.multiple_of(c * step, step), step)
            part = rows[side, q, :, :, at].reshape(2 * block, step)
            acc[:, : 2 * HD] += jnp.dot(part, r.w_query[at, :], preferred_element_type=F32)
            acc[:, 2 * HD :] += dotg(part, r.kv_out[:, at], NT)
            return 0

        lax.fori_loop(0, width // step, body, 0)
        scale = width ** (-0.5)
        here = pl.ds(pl.multiple_of((side * 4 + q) * 2 * block, 2 * block), 2 * block)
        cos, sin = r.cos[here, :], r.sin[here, :]
        for h in range(2):
            r.query[here, h * HD : (h + 1) * HD] = rope(
                acc[:, h * HD : (h + 1) * HD] * scale, cos, sin, 1.0
            ).astype(BF)
        r.key[here, :] = rope(acc[:, 2 * HD : 3 * HD] * scale, cos, sin, 1.0).astype(BF)
        r.value[here, :] = (acc[:, 3 * HD :] * scale).astype(BF)

    link.wait(kv_slots[0], kv_piece(other)(z), pair)
    sides = lambda ref, i: ref.at[:, pl.ds(i * (width // 2), width // 2)]
    kv_ring = ring_spread(link, z, z_up, z_down, kv_piece(other), sides)
    next(kv_ring)
    next(kv_ring)
    finish(kv_ring)
    link.start(kv_slots[2], kv.at[other], kv.at[other], sib)
    placed.wait()
    moment_slot = link.slot()
    link.start(moment_slot, here, here, beside)
    half = r.moment_own.shape[0] // 2
    parts = lambda ref, i: ref.at[pl.ds(i * half, half)]
    near_moments = ring_spread(
        link, z, z_up, z_down, lambda q: moments.at[xl * 4 + q], parts
    )
    far_moments = ring_spread(
        link, z, z_up, z_down, lambda q: moments.at[(1 - xl) * 4 + q], parts
    )
    next(near_moments)
    crossed(top_slot, q0, top)
    a_far = spread(1 - xh, top, LOW_FRONT)
    next(a_far)
    next(b_own)
    cross(rest_slots[1], q1, rest)
    cross(rest_slots[3], q3, rest)
    next(a_own)
    to_sib(sib_slots[0][1], xh, q1)
    to_sib(sib_slots[0][3], xh, q3)
    crossed(rest_slots[0], q0, rest)
    to_sib(sib_slots[1][0], 1 - xh, q0)
    finish(b_own)
    cross(rest_slots[2], q2, rest)
    finish(a_own)
    to_sib(sib_slots[0][2], xh, q2)
    next(a_far)
    link.wait(kv_slots[1], kv.at[odd * 2 + 1 - core], sib)
    link.wait(kv_slots[2], kv.at[(1 - odd) * 2 + 1 - core], sib)
    for j in range(INNER):
        r.kv_out[j * thin : (j + 1) * thin, :] = kv[j, :thin, :]
        r.kv_out[HD + j * thin : HD + (j + 1) * thin, :] = kv[j, thin:, :]
    next(near_moments)
    link.wait(moment_slot, moments.at[(1 - xl) * 4 + z], beside)
    next(far_moments)
    project(xh, q0, 0)
    project(xh, q1, 1)
    project(xh, q3, 3)
    project(1 - xh, q0, 4)
    project(xh, q2, 2)
    finish(a_far)
    crossed(rest_slots[1], q1, rest)
    to_sib(sib_slots[1][1], 1 - xh, q1)
    crossed(rest_slots[3], q3, rest)
    to_sib(sib_slots[1][3], 1 - xh, q3)
    crossed(rest_slots[2], q2, rest)
    to_sib(sib_slots[1][2], 1 - xh, q2)
    next(far_moments)
    finish(near_moments)
    project(1 - xh, q1, 5)
    project(1 - xh, q3, 7)
    project(1 - xh, q2, 6)
    finish(far_moments)
    link.wait(kv_slots[3], r.w_other, sib)
    for copy in stored:
        copy.wait()
    link.drain()


def front(tokens, gain, w_query, kv_own, cos, sin, moment_own):
    block, width = tokens.shape
    length = cos.shape[0]
    v = pltpu.VMEM
    shape = jax.ShapeDtypeStruct
    ins = dict(
        tokens=tokens,
        gain=gain,
        w_query=w_query,
        kv_own=kv_own,
        cos=cos,
        sin=sin,
        moment_own=moment_own,
    )
    outs = dict(
        query=shape((length, 2 * HD), BF),
        key=shape((length, HD), BF),
        value=shape((length, HD), BF),
        rows_out=shape((2, 4, 2, block, width), BF),
        w_other=shape(w_query.shape, BF),
        kv_out=shape((2 * HD, width), BF),
        moment_all=shape((8, *moment_own.shape), BF),
    )
    scratch = dict(
        rows=v((2, 4, 2, block, width), BF),
        kv=v((INNER, 2 * HD // INNER, width), BF),
        acc=v((2 * block, 4 * HD), F32),
        store=pltpu.SemaphoreType.DMA((9,)),
        send=pltpu.SemaphoreType.DMA((48,)),
        recv=pltpu.SemaphoreType.DMA((48,)),
    )
    whole = pl.BlockSpec(memory_space=pltpu.VMEM)
    far = pl.BlockSpec(memory_space=pl.ANY)
    return pl.pallas_call(
        functools.partial(front_kernel, tuple(ins) + tuple(outs) + tuple(scratch)),
        in_specs=[whole] * len(ins),
        out_specs=[whole, whole, whole, far, far, whole, far],
        out_shape=list(outs.values()),
        scratch_shapes=list(scratch.values()),
        compiler_params=pltpu.CompilerParams(
            collective_id=2, has_side_effects=True, vmem_limit_bytes=60 * 1024 * 1024
        ),
        name="front",
    )(*ins.values())


def tables(length):
    within = np.arange(HD) // 2
    rates = np.power(np.float32(rope_base), within.astype(np.float32) * np.float32(-2.0 / HD))
    angle = np.arange(length, dtype=np.float32)[:, None] * rates.astype(np.float32)[None, :]
    angle = angle.astype(np.float64)
    return np.cos(angle).astype(np.float32), np.sin(angle).astype(np.float32)


def per_device(
    tokens, cotangent, gain, w_query, w_key, w_value, moment_query, moment_key, moment_value
):
    key_width = w_key.shape[1]
    width = tokens.shape[2]
    cos, sin = tables(cotangent.shape[1])
    kv_own = jnp.concatenate([w_key, w_value], axis=1).T
    moment_kv = jnp.concatenate([moment_key, moment_value], axis=1).T
    halves = jnp.split(moment_kv, 2, axis=1)
    moment_own = jnp.concatenate([moment_query, *halves], axis=0).astype(BF)
    query, key, value, rows, w_other, w_head, moment_all = front(
        tokens[0], gain[None], w_query, kv_own, cos, sin, moment_own
    )
    length = query.shape[0]
    rows = rows.reshape(length, width)
    attended, grad_query, grad_kv = attention(query, key, value, cotangent[0], cos, sin)
    by_block = (8, 2, length // 16, 2 * HD)
    grad_tokens, fresh_query, fresh_kv, next_query, next_kv = back(
        grad_query.reshape(by_block),
        grad_kv.reshape(by_block),
        w_query,
        w_other,
        w_head,
        kv_own,
        tokens[0],
        gain[None],
        rows,
        moment_query,
        moment_kv,
        moment_all,
    )
    fresh_key, fresh_value = fresh_kv[:key_width].T, fresh_kv[key_width:].T
    next_key, next_value = next_kv[:key_width].T, next_kv[key_width:].T
    return (
        attended[None],
        grad_tokens[None],
        fresh_query,
        fresh_key,
        fresh_value,
        next_query,
        next_key,
        next_value,
    )


def solution(mesh):
    torus = Mesh(mesh.devices.reshape(2, 4, 2, 2, 2, 2), ALL)
    placed = (
        P(DP, TENSOR, None),
        P(DP, None, TENSOR),
        P(),
        P(None, TENSOR),
        P(None, TENSOR),
        P(None, TENSOR),
        P(DP, TENSOR),
        P(DP, TENSOR),
        P(DP, TENSOR),
    )
    return jax.shard_map(
        per_device,
        mesh=torus,
        in_specs=placed,
        out_specs=(
            P(DP, None, TENSOR),
            P(DP, TENSOR, None),
            P(None, TENSOR),
            P(None, TENSOR),
            P(None, TENSOR),
            P(DP, TENSOR),
            P(DP, TENSOR),
            P(DP, TENSOR),
        ),
        check_vma=False,
    )
```
